128 devices in a mesh: row: 32 (over z, y, core), ch: 4 (over x).
Axes of the slice: x: 4, y: 4, z: 4, core: 2. Of those that a mesh axis runs over, the one named last changes fastest.
Arguments:
- pair_act: bfloat16 [512, 512, 128], P('row', 'ch'), may hold values from -6 to 6
- valid_count: int32 [1], replicated, may hold values from 257 to 512
- edge_proj: bfloat16 [128, 256], replicated, may hold values from -0.5 to 0.5
- edge_gate: bfloat16 [128, 256], replicated, may hold values from -0.5 to 0.5
- tri_gate: bfloat16 [128, 128], replicated, may hold values from -0.5 to 0.5
- tri_out: bfloat16 [128, 128], replicated, may hold values from -0.5 to 0.5
- attn_proj: bfloat16 [128, 512], replicated, may hold values from -0.5 to 0.5
- bias_proj: bfloat16 [128, 4], replicated, may hold values from -24 to 24, as said below
- attn_out: bfloat16 [128, 128], replicated, may hold values from -0.5 to 0.5
Outputs:
- pair_out: bfloat16 [512, 512, 128], P('row', 'ch')
The draws below stay inside these ranges and needn't reach their ends.
Inputs may be any that keep to these rules, and one draw needn't show every extreme that they name: `bias_proj`: biases' projection; its columns differ in scale.
All inputs are finite; a program needn't handle non-finite values.
Results may differ from the reference program's by a relative error of at most 0.038.
Values may be sent and summed in bfloat16 or wider, within the bound.
A program may use at most 128 MiB of HBM per device.

```python
import math
import jax
import jax.numpy as jnp
from jax import lax

C = 128
HEADS = 4
HEAD_DIM = 32
TOKENS = 512


def draw_bias_proj(key, part):
    key = jax.random.fold_in(key, 11)
    base = jnp.clip(jax.random.normal(key, (C, HEADS), jnp.float32), -4.0, 4.0) * C ** (-0.5)
    factors = jnp.exp(jax.random.uniform(jax.random.fold_in(key, 1), (HEADS,), jnp.float32, 0.0, math.log(3.0)))
    return (base * factors[None, :]).astype(jnp.bfloat16)


def levels(key, shape, shards, low, top_value):
    def one(dim, blocks):
        draws = jax.random.uniform(jax.random.fold_in(jax.random.fold_in(key, 6), dim), (blocks,), jnp.float32, low / len(shards), top_value / len(shards))
        return jnp.repeat(jnp.exp(draws), shape[dim] // blocks).reshape((-1,) + (1,) * (len(shape) - dim - 1))

    gain = one(*shards[0])
    for cut in shards[1:]:
        gain = gain * one(*cut)
    return gain


def centred(stream_key, dims, width, most, cuts=(), dtype=jnp.bfloat16):
    factor_of = levels(stream_key, dims, cuts, -0.22, 0.18) if cuts else 1.0
    array = jax.random.normal(stream_key, dims, jnp.float32) * width * factor_of
    return jnp.minimum(jnp.maximum(array, -most), most).astype(dtype)


def setup_inputs(seed: int = 0) -> dict:
    seeds = jax.random.split(jax.random.key(seed), 10)
    pair_act = centred(seeds[0], (TOKENS, TOKENS, C), 1.0, 6.0, ((0, 32), (1, 4)))
    valid_count = jax.random.randint(seeds[1], (1,), TOKENS // 2 + 1, TOKENS + 1).astype(jnp.int32)
    edge_proj = centred(seeds[2], (C, 2 * C), C ** -0.5, 0.5)
    edge_gate = centred(seeds[3], (C, 2 * C), C ** -0.5, 0.5)
    tri_gate = centred(seeds[4], (C, C), C ** -0.5, 0.5)
    tri_out = centred(seeds[5], (C, C), C ** -0.5, 0.5)
    attn_proj = centred(seeds[6], (C, 4 * C), C ** -0.5, 0.5)
    bias_proj = draw_bias_proj(jax.random.fold_in(seeds[9], 71), 0)
    attn_out = centred(seeds[8], (C, C), C ** -0.5, 0.5)
    return dict(pair_act=pair_act, valid_count=valid_count, edge_proj=edge_proj, edge_gate=edge_gate, tri_gate=tri_gate, tri_out=tri_out, attn_proj=attn_proj, bias_proj=bias_proj, attn_out=attn_out)


EPS = 1e-05

def layer_norm(values):
    centre = values - lax.optimization_barrier(jnp.mean(values, axis=-1, keepdims=True))
    spread = lax.optimization_barrier(jnp.mean(centre * centre, axis=-1, keepdims=True))
    return centre * lax.rsqrt(spread + EPS)

def reference(pair_act, valid_count, edge_proj, edge_gate, tri_gate, tri_out, attn_proj, bias_proj, attn_out):
    length = valid_count[0]
    token_valid = (jnp.arange(TOKENS) < length).astype(jnp.float32)
    pair_valid = token_valid[:, None] * token_valid[None, :]
    source = pair_act.astype(jnp.float32)
    normed = layer_norm(source).astype(jnp.bfloat16)
    projected = jnp.dot(normed, edge_proj, preferred_element_type=jnp.float32)
    gating = jnp.dot(normed, edge_gate, preferred_element_type=jnp.float32)
    edges = (jax.nn.sigmoid(gating) * projected * pair_valid[:, :, None]).astype(jnp.bfloat16)
    left_edges = edges[:, :, :C].astype(jnp.float32)
    right_edges = edges[:, :, C:].astype(jnp.float32)
    triangle = jnp.einsum('ikc,jkc->ijc', left_edges, right_edges)
    tri_normed = layer_norm(triangle).astype(jnp.bfloat16)
    update = jax.nn.sigmoid(jnp.dot(normed, tri_gate, preferred_element_type=jnp.float32)) * jnp.dot(tri_normed, tri_out, preferred_element_type=jnp.float32)
    updated = (source + update).astype(jnp.bfloat16)
    attn_normed = layer_norm(updated.astype(jnp.float32)).astype(jnp.bfloat16)
    mixed = jnp.dot(attn_normed, attn_proj, preferred_element_type=jnp.float32)
    query = mixed[..., :C].astype(jnp.bfloat16)
    keys = mixed[..., C:2 * C].astype(jnp.bfloat16)
    values = mixed[..., 2 * C:3 * C].astype(jnp.bfloat16)
    attn_gate = jax.nn.sigmoid(mixed[..., 3 * C:])
    head_bias = jnp.transpose(jnp.dot(attn_normed, bias_proj, preferred_element_type=jnp.float32), (2, 0, 1)).astype(jnp.bfloat16)
    bias_float = head_bias.astype(jnp.float32)
    key_term = (token_valid - 1.0) * 1000000000.0
    score_scale = HEAD_DIM ** (-0.5)
    group = 16

    def attend(block):
        query_rows, key_rows, value_rows = block
        query_heads = query_rows.astype(jnp.float32).reshape(group, TOKENS, HEADS, HEAD_DIM)
        key_heads = key_rows.astype(jnp.float32).reshape(group, TOKENS, HEADS, HEAD_DIM)
        value_heads = value_rows.astype(jnp.float32).reshape(group, TOKENS, HEADS, HEAD_DIM)
        logits = jnp.einsum('ijhd,ikhd->ihjk', query_heads, key_heads) * score_scale
        logits = logits + bias_float[None] + key_term[None, None, None, :]
        attn_weights = jax.nn.softmax(logits, axis=-1).astype(jnp.bfloat16)
        output = jnp.einsum('ihjk,ikhd->ijhd', attn_weights.astype(jnp.float32), value_heads)
        return output.reshape(group, TOKENS, C)
    blocks = TOKENS // group
    attended = lax.map(attend, (query.reshape(blocks, group, TOKENS, C), keys.reshape(blocks, group, TOKENS, C), values.reshape(blocks, group, TOKENS, C)))
    attended = attended.reshape(TOKENS, TOKENS, C)
    gated = (attended * attn_gate).astype(jnp.bfloat16)
    return (updated.astype(jnp.float32) + jnp.dot(gated, attn_out, preferred_element_type=jnp.float32)).astype(jnp.bfloat16)
```

```python
import functools
import math

import jax
import jax.numpy as jnp
from jax import lax
from jax.experimental import pallas as pl
from jax.experimental.pallas import tpu as pltpu
from jax.sharding import PartitionSpec as P

MESH = pl.DeviceIdType.MESH
EPS = 1e-05
F32 = jnp.float32
BF16 = jnp.bfloat16
LOG2E = math.log2(math.e)
NT = (((1,), (1,)), ((), ()))
NN = (((1,), (0,)), ((), ()))

LINE = 4
ROWS = 16
COLS = 128
CH = 128
TOK = 512
HEADS = 4
HEAD = 32
OWN = 4
DEVICES = 128


def dot(a, b, dims=NN):
    return lax.dot_general(a, b, dims, preferred_element_type=F32)


def sigmoid(x):
    return 0.5 * jnp.tanh(0.5 * x) + 0.5


def layer_norm(x):
    centre = x - jnp.mean(x, axis=-1, keepdims=True)
    spread = jnp.mean(centre * centre, axis=-1, keepdims=True)
    return centre * lax.rsqrt(spread + EPS)


def kernel(
    count_ref, pa, ep, eg, tg, to, ap, bp, ao,
    out,
    wt, ebuf, esend, lr, tst, tsend, trecv, tn, gbuf, a2, upd, an, qs, ks, vs, gs, bg, bias, osend,
    pa_send, pa_recv, pa_own, e_send, e_recv, t_send, t_recv,
    bx_send, bx_recv, by_send, by_recv, bz_send, bz_recv, bc_send, bc_recv, o_send, o_recv,
):
    r = lax.axis_index("row")
    q = lax.axis_index("ch")
    me = r * LINE + q
    z = lax.div(r, 8)
    y = lax.rem(lax.div(r, 2), 4)
    core = lax.rem(r, 2)
    count = count_ref[0]

    def place(zz, yy, cc):
        return zz * 8 + yy * 2 + cc

    def peer(step):
        t = lax.rem(step * 37, DEVICES)
        qq = lax.rem(q + lax.rem(t, 4), 4)
        cc = lax.rem(core + lax.rem(lax.div(t, 4), 2), 2)
        yy = lax.rem(y + lax.rem(lax.div(t, 8), 4), 4)
        zz = lax.rem(z + lax.div(t, 32), 4)
        return place(zz, yy, cc), qq

    def remote(src, dst, send, recv, rr, qq):
        return pltpu.make_async_remote_copy(
            src_ref=src, dst_ref=dst, send_sem=send, recv_sem=recv,
            device_id=(rr, qq), device_id_type=MESH,
        )

    def settle(ref, sem):
        pltpu.make_async_copy(ref, ref, sem).wait()

    barrier = pltpu.get_barrier_semaphore()

    @pl.loop(1, DEVICES)
    def _(step):
        rr, qq = peer(step)
        pl.semaphore_signal(barrier, inc=1, device_id=(rr, qq), device_id_type=MESH)

    wt[0:256, :] = ep[...].astype(F32).T.astype(BF16)
    wt[256:512, :] = eg[...].astype(F32).T.astype(BF16)
    lane = lax.broadcasted_iota(jnp.int32, (1, 256), 1)

    @pl.loop(0, ROWS // 2)
    def _(pair):
        x = pa[pl.ds(pair * 2, 2)].reshape(256, CH).astype(F32)
        normed = layer_norm(x).astype(BF16)
        both = dot(wt[...], normed, NT)
        row_token = r * ROWS + pair * 2 + lane // 128
        col_token = q * COLS + lane % 128
        valid = jnp.where((row_token < count) & (col_token < count), 1.0, 0.0)
        edges = sigmoid(both[256:512]) * both[0:256] * valid
        for side in range(2):
            for k in range(2):
                ebuf[pl.ds(side * 16 + pair * 2 + k, 128, stride=32), :] = edges[
                    side * 128 : side * 128 + 128, k * 128 : k * 128 + 128
                ]

    @pl.loop(0, 8)
    def _(part):
        rows = pl.ds(pl.multiple_of(part * 512, 512), 512)
        esend[rows, :] = ebuf[rows, :].astype(BF16)

    pl.semaphore_wait(barrier, DEVICES - 1)

    @pl.loop(1, DEVICES)
    def _(step):
        rr, qq = peer(step)
        rows = pl.ds(pl.multiple_of((rr * LINE + qq) * 32, 32), 32)
        remote(esend.at[rows], lr.at[q, r], e_send, e_recv, rr, qq).start()

    own = pl.ds(pl.multiple_of(me * 32, 32), 32)
    pltpu.make_async_copy(esend.at[own], lr.at[q, r], e_recv).start()

    pa_copies = []
    for dq in range(1, LINE):
        qq = lax.rem(q + dq, LINE)
        copy = remote(
            pa.at[pl.ds(qq * OWN, OWN)], a2.at[q], pa_send.at[dq - 1], pa_recv.at[dq - 1], r, qq
        )
        copy.start()
        pa_copies.append(copy)
    pa_local = pltpu.make_async_copy(pa.at[pl.ds(q * OWN, OWN)], a2.at[q], pa_own)
    pa_local.start()

    settle(lr, e_recv)
    right = jnp.concatenate([lr[k, :, 16:32, :].reshape(TOK, COLS) for k in range(LINE)], axis=1)
    for half in range(2):
        left = jnp.concatenate(
            [lr[k, half * 16 : half * 16 + 16, 0:16, :].reshape(256, COLS) for k in range(LINE)],
            axis=1,
        )
        tri = dot(left, right, NT)
        for jb in range(LINE):
            tst[pl.ds(half * 1024 + jb, 256, stride=4), :] = tri[:, jb * 128 : jb * 128 + 128]

    @pl.loop(0, 4)
    def _(part):
        rows = pl.ds(pl.multiple_of(part * 512, 512), 512)
        tsend[rows, :] = tst[rows, :].astype(BF16)

    @pl.loop(1, DEVICES)
    def _(step):
        rr, qq = peer(step)
        rows = pl.ds(pl.multiple_of((rr * LINE + qq) * 16, 16), 16)
        remote(tsend.at[rows], trecv.at[me], t_send, t_recv, rr, qq).start()

    own = pl.ds(pl.multiple_of(me * 16, 16), 16)
    pltpu.make_async_copy(tsend.at[own], trecv.at[me], t_recv).start()

    pa_local.wait()
    for copy in pa_copies:
        copy.wait()

    @pl.loop(0, OWN)
    def _(il):
        x = a2[:, il].reshape(TOK, CH).astype(F32)
        gbuf[il] = sigmoid(dot(layer_norm(x).astype(BF16), tg[...]))

    settle(trecv, t_recv)

    def add(part, total):
        return total + jnp.sum(trecv[pl.ds(part * 16, 16)].astype(F32), axis=0)

    mean = lax.fori_loop(0, 8, add, jnp.zeros((16, 128), F32)) * (1.0 / CH)

    def add_square(part, total):
        centre = trecv[pl.ds(part * 16, 16)].astype(F32) - mean[None]
        return total + jnp.sum(centre * centre, axis=0)

    spread = lax.fori_loop(0, 8, add_square, jnp.zeros((16, 128), F32)) * (1.0 / CH)
    gain = lax.rsqrt(spread + EPS)

    @pl.loop(0, 8)
    def _(part):
        block = (trecv[pl.ds(part * 16, 16)].astype(F32) - mean[None]) * gain[None]
        tn[pl.ds(pl.multiple_of(part * 256, 256), 256), :] = block.reshape(256, 128)

    spot = lax.broadcasted_iota(jnp.int32, (16, HEADS), 0) % HEADS
    pick = (spot == lax.broadcasted_iota(jnp.int32, (16, HEADS), 1)).astype(BF16)
    bias_w = dot(pick, bp[...], NT).astype(BF16)
    bias_row = lax.broadcasted_iota(jnp.int32, (16, TOK), 0) // HEADS

    def update(il, own_bias):
        blocks = [
            tn[pl.ds(il * LINE + jb, 128, stride=16), :].T.astype(BF16) for jb in range(LINE)
        ]
        product = dot(jnp.concatenate(blocks, axis=0), to[...])
        x = a2[:, il].reshape(TOK, CH).astype(F32)
        updated = (x + gbuf[il] * product).astype(BF16)
        upd[il] = updated
        normed = layer_norm(updated.astype(F32)).astype(BF16)
        an[il] = normed
        return jnp.where(bias_row == il, dot(bias_w, normed, NT), own_bias)

    own_bias = lax.fori_loop(0, OWN, update, jnp.zeros((16, TOK), F32)).astype(BF16)
    for kb in range(LINE):
        bg[z, core, y, q, kb * 16 : kb * 16 + 16, :] = own_bias[:, kb * 128 : kb * 128 + 128]

    sends = []
    for dq in range(1, LINE):
        copy = remote(
            bg.at[z, core, y, q], bg.at[z, core, y, q], bx_send.at[dq - 1], bx_recv.at[dq - 1],
            r, lax.rem(q + dq, LINE),
        )
        copy.start()
        sends.append(copy)

    def project(il):
        mixed = dot(an[il], ap[...])
        qs[il] = (mixed[:, 0:CH] * (HEAD**-0.5 * LOG2E)).astype(BF16)
        ks[il] = mixed[:, CH : 2 * CH].astype(BF16)
        vs[il] = mixed[:, 2 * CH : 3 * CH].astype(BF16)
        gs[il] = sigmoid(mixed[:, 3 * CH : 4 * CH])

    @pl.loop(0, 2)
    def _(il):
        project(il)

    for dq in range(1, LINE):
        slot = bg.at[z, core, y, lax.rem(q + LINE - dq, LINE)]
        settle(slot, bx_recv.at[dq - 1])
    twin = place(z, y, 1 - core)
    for dy in range(1, LINE):
        copy = remote(
            bg.at[z, core, y], bg.at[z, core, y], by_send.at[dy - 1], by_recv.at[dy - 1],
            place(z, lax.rem(y + dy, LINE), core), q,
        )
        copy.start()
        sends.append(copy)
    copy = remote(bg.at[z, core, y], bg.at[z, core, y], bc_send.at[0], bc_recv.at[0], twin, q)
    copy.start()
    sends.append(copy)

    @pl.loop(2, OWN)
    def _(il):
        project(il)

    for dy in range(1, LINE):
        yy = lax.rem(y + LINE - dy, LINE)
        settle(bg.at[z, core, yy], by_recv.at[dy - 1])
        copy = remote(
            bg.at[z, core, yy], bg.at[z, core, yy], bc_send.at[dy], bc_recv.at[dy], twin, q
        )
        copy.start()
        sends.append(copy)
    for dz in range(1, LINE):
        copy = remote(
            bg.at[z, core], bg.at[z, core], bz_send.at[dz - 1], bz_recv.at[dz - 1],
            place(lax.rem(z + dz, LINE), y, core), q,
        )
        copy.start()
        sends.append(copy)
    for dy in range(LINE):
        settle(bg.at[z, 1 - core, lax.rem(y + LINE - dy, LINE)], bc_recv.at[dy])

    key_lane = lax.broadcasted_iota(jnp.int32, (1, TOK), 1)
    key_term = jnp.where(key_lane < count, 0.0, -1e9 * LOG2E)
    head_of = lax.broadcasted_iota(jnp.int32, (128, CH), 1) // HEAD

    def forward(dz):
        zz = lax.rem(z + LINE - dz, LINE)
        return remote(
            bg.at[zz, core], bg.at[zz, core], bc_send.at[3 + dz], bc_recv.at[3 + dz], twin, q
        )

    @pl.loop(0, LINE)
    def _(step):
        jb = lax.rem(z + LINE - step, LINE)

        @pl.when(step > 0)
        def _():
            settle(bg.at[jb, 1 - core], bc_recv.at[3 + step])

        @pl.loop(0, LINE)
        def _(yy):
            for cc in range(2):
                for xx in range(LINE):
                    rows = pl.ds(pl.multiple_of(yy * 128 + cc * 64 + xx * 16, 16), 16)
                    tile = bg[jb, cc, yy, xx].astype(F32)
                    for kb in range(LINE):
                        cols = slice(kb * 128, kb * 128 + 128)
                        bias[kb, rows, :] = tile[kb * 16 : kb * 16 + 16] * LOG2E + key_term[:, cols]

        @pl.loop(0, OWN)
        def _(il):
            @pl.when((il == 2) & (step < LINE - 1))
            def _():
                zz = lax.rem(z + LINE - 1 - step, LINE)
                settle(bg.at[zz, core], bz_recv.at[step])
                forward(step + 1).start()

            block = pl.ds(pl.multiple_of(jb * 128, 128), 128)
            query = qs[il, block, :]
            masked = [jnp.where(head_of == h, query, jnp.zeros_like(query)) for h in range(HEADS)]
            scores = dot(jnp.concatenate(masked, axis=0), ks[il], NT)
            weights = []
            scale = []
            for h in range(HEADS):
                own = [bias[kb, pl.ds(h, 128, stride=4), :] for kb in range(LINE)]
                logits = scores[h * 128 : h * 128 + 128] + jnp.concatenate(own, axis=1)
                powers = jnp.exp2(logits - jnp.max(logits, axis=-1, keepdims=True))
                scale.append(1.0 / jnp.sum(powers, axis=-1, keepdims=True))
                weights.append(powers.astype(BF16))
            mixed = dot(jnp.concatenate(weights, axis=0), vs[il])
            attended = jnp.zeros((128, CH), F32)
            for h in range(HEADS):
                attended = jnp.where(head_of == h, mixed[h * 128 : h * 128 + 128] * scale[h], attended)
            gated = (attended * gs[il, block, :]).astype(BF16)
            result = upd[il, block, :].astype(F32) + dot(gated, ao[...])
            osend[jb, il] = result.astype(BF16)

            target = out.at[q * OWN + il]

            @pl.when(jb != q)
            def _():
                remote(osend.at[jb, il], target, o_send, o_recv, r, jb).start()

            @pl.when(jb == q)
            def _():
                pltpu.make_async_copy(osend.at[jb, il], target, o_recv).start()

    settle(out, o_recv)
    settle(osend.at[0:3], o_send)
    settle(esend.at[0 : 32 * (DEVICES - 1)], e_send)
    settle(tsend.at[0 : 16 * (DEVICES - 1)], t_send)
    for copy in sends:
        copy.wait_send()
    for dz in range(1, LINE):
        forward(dz).wait_send()


def local(pair_act, valid_count, edge_proj, edge_gate, tri_gate, tri_out, attn_proj, bias_proj, attn_out):
    vmem = pl.BlockSpec(memory_space=pltpu.VMEM)
    dma = pltpu.SemaphoreType.DMA
    return pl.pallas_call(
        kernel,
        out_shape=jax.ShapeDtypeStruct((ROWS, COLS, CH), BF16),
        in_specs=[pl.BlockSpec(memory_space=pltpu.SMEM)] + [vmem] * 8,
        out_specs=pl.BlockSpec(memory_space=pl.ANY),
        scratch_shapes=[
            pltpu.VMEM((512, CH), BF16),
            pltpu.VMEM((4096, COLS), F32),
            pltpu.VMEM((4096, COLS), BF16),
            pltpu.VMEM((LINE, 32, 32, COLS), BF16),
            pltpu.VMEM((2048, 128), F32),
            pltpu.VMEM((2048, 128), BF16),
            pltpu.VMEM((CH, 16, 128), BF16),
            pltpu.VMEM((2048, 128), F32),
            pltpu.VMEM((OWN, TOK, CH), F32),
            pltpu.VMEM((LINE, OWN, COLS, CH), BF16),
            pltpu.VMEM((OWN, TOK, CH), BF16),
            pltpu.VMEM((OWN, TOK, CH), BF16),
            pltpu.VMEM((OWN, TOK, CH), BF16),
            pltpu.VMEM((OWN, TOK, CH), BF16),
            pltpu.VMEM((OWN, TOK, CH), BF16),
            pltpu.VMEM((OWN, TOK, CH), F32),
            pltpu.VMEM((LINE, 2, LINE, LINE, 64, 128), BF16),
            pltpu.VMEM((LINE, 512, 128), F32),
            pltpu.VMEM((LINE, OWN, 128, CH), BF16),
            dma((3,)), dma((3,)), dma, dma, dma, dma, dma,
            dma((3,)), dma((3,)), dma((3,)), dma((3,)), dma((3,)), dma((3,)), dma((7,)), dma((7,)),
            dma, dma,
        ],
        compiler_params=pltpu.CompilerParams(
            collective_id=0, has_side_effects=True, vmem_limit_bytes=48 * 1024 * 1024
        ),
        name="triangle",
    )(valid_count, pair_act, edge_proj, edge_gate, tri_gate, tri_out, attn_proj, bias_proj, attn_out)


def solution(mesh):
    placed = (P("row", "ch", None), P(), P(), P(), P(), P(), P(), P(), P())
    return jax.shard_map(
        local, mesh=mesh, in_specs=placed, out_specs=P("row", "ch", None), check_vma=False
    )
```

```python
import math

import jax
import jax.numpy as jnp
from jax import lax
from jax.experimental import pallas as pl
from jax.experimental.pallas import tpu as pltpu
from jax.sharding import PartitionSpec as P

MESH = pl.DeviceIdType.MESH
EPS = 1e-05
F32 = jnp.float32
BF16 = jnp.bfloat16
LOG2E = math.log2(math.e)
NT = (((1,), (1,)), ((), ()))
NN = (((1,), (0,)), ((), ()))

LINE = 4
ROWS = 16
COLS = 128
CH = 128
TOK = 512
HEADS = 4
HEAD = 32
OWN = 4
DEVICES = 128


OFFSETS = [
    (dz, dy, dc, dx) for dz in range(LINE) for dy in range(LINE) for dc in range(2) for dx in range(LINE)
][1:]


def hops(offset):
    dz, dy, _, dx = offset
    return sum(min(d, LINE - d) for d in (dz, dy, dx))


FAR_FIRST = sorted(OFFSETS, key=hops, reverse=True)


def dot(a, b, dims=NN):
    return lax.dot_general(a, b, dims, preferred_element_type=F32)


def sigmoid(x):
    return 0.5 * jnp.tanh(0.5 * x) + 0.5


def layer_norm(x):
    centre = x - jnp.mean(x, axis=-1, keepdims=True)
    spread = jnp.mean(centre * centre, axis=-1, keepdims=True)
    return centre * lax.rsqrt(spread + EPS)


def kernel(
    count_ref, pa_in, ep_in, eg_in, tg_in, to_in, ap_in, bp_in, ao_in,
    out,
    pa, ep, eg, tg, to, ap, bp, ao, wt, nrm, ebuf, esend, lr, tst, tsend, trecv, tn, gbuf, a2, upd, an, qs, ks, vs, gs, ba, bb, bc, sbuf, bias, osend,
    ready, load, pa_send, pa_recv, pa_own, e_send, e_recv, t_send, t_recv,
    b_send, b_recv, u_send, u_recv, o_send, o_recv,
):
    r = lax.axis_index("row")
    q = lax.axis_index("ch")
    me = r * LINE + q
    z = lax.div(r, 8)
    y = lax.rem(lax.div(r, 2), 4)
    core = lax.rem(r, 2)
    count = count_ref[0]

    def place(zz, yy, cc):
        return zz * 8 + yy * 2 + cc

    zs = [lax.rem(z + d, LINE) for d in range(LINE)]
    ys = [lax.rem(y + d, LINE) for d in range(LINE)]
    xs = [lax.rem(q + d, LINE) for d in range(LINE)]
    cores = [core, 1 - core]

    def peer(offset):
        dz, dy, dc, dx = offset
        return place(zs[dz], ys[dy], cores[dc]), xs[dx]

    def remote(src, dst, send, recv, rr, qq):
        return pltpu.make_async_remote_copy(
            src_ref=src, dst_ref=dst, send_sem=send, recv_sem=recv,
            device_id=(rr, qq), device_id_type=MESH,
        )

    def settle(ref, sem):
        pltpu.make_async_copy(ref, ref, sem).wait()

    loads = [
        pltpu.make_async_copy(src, dst, load.at[n])
        for n, (src, dst) in enumerate(
            [(ep_in, ep), (eg_in, eg), (pa_in, pa), (tg_in, tg), (to_in, to), (ap_in, ap), (bp_in, bp), (ao_in, ao)]
        )
    ]
    for copy in loads:
        copy.start()

    barrier = pltpu.get_barrier_semaphore()

    plane = [o for o in OFFSETS if o[2] == 0 and o[3] == 0]
    near = [o for o in OFFSETS if o[0] == 0 and o[1] == 0] + plane
    for offset in near:
        rr, qq = peer(offset)
        pl.semaphore_signal(barrier, inc=1, device_id=(rr, qq), device_id_type=MESH)

    for copy in loads:
        copy.wait()

    @pl.loop(0, 4)
    def _(part):
        x = pa[pl.ds(part * 4, 4)].reshape(512, CH).astype(F32)
        nrm[pl.ds(pl.multiple_of(part * 512, 512), 512), :] = layer_norm(x).astype(BF16)

    pl.semaphore_wait(barrier, len(near))
    for offset in plane:
        rr, qq = peer(offset)
        pl.semaphore_signal(ready, inc=1, device_id=(rr, qq), device_id_type=MESH)

    spot = lax.broadcasted_iota(jnp.int32, (CH, CH), 0)
    line = spot % 32
    chosen = line * 4 + (spot // 32 + 8 - line // 8 - (line // 2) % 4) % 4
    order = (chosen == lax.broadcasted_iota(jnp.int32, (CH, CH), 1)).astype(BF16)
    for n, ref in enumerate((ep, ep, eg, eg)):
        side = n % 2
        part = dot(order, ref[:, side * CH : side * CH + CH], NT).astype(BF16)
        for m in range(4):
            wt[m, n * 32 : n * 32 + 32, :] = part[m * 32 : m * 32 + 32]
    lane = lax.broadcasted_iota(jnp.int32, (1, 512), 1)

    def edges_of(k):
        weights = wt[lax.rem(z + y + q + k, 4)]
        for part in range(4):
            both = dot(weights, nrm[part * 512 : part * 512 + 512, :], NT)
            row_token = r * ROWS + part * 4 + lane // 128
            col_token = q * COLS + lane % 128
            valid = jnp.where((row_token < count) & (col_token < count), 1.0, 0.0)
            edges = sigmoid(both[64:128]) * both[0:64] * valid
            for i in range(4):
                for side in range(2):
                    ebuf[pl.ds(side * 16 + part * 4 + i, 32, stride=36), :] = edges[
                        side * 32 : side * 32 + 32, i * 128 : i * 128 + 128
                    ]
        for n in range(32):
            esend[k, n * 32 : n * 32 + 32, :] = ebuf[n * 36 : n * 36 + 32, :].astype(BF16)

    for step, k in enumerate((2, 1, 3, 0)):
        edges_of(k)
        if step == 0:
            pl.semaphore_wait(ready, len(plane))
        for offset in FAR_FIRST:
            if (offset[0] + offset[1] + offset[3]) % 4 == k:
                rr, qq = peer(offset)
                rows = pl.ds(pl.multiple_of(rr * 32, 32), 32)
                remote(esend.at[k, rows], lr.at[q, r], e_send, e_recv, rr, qq).start()

    own = pl.ds(pl.multiple_of(r * 32, 32), 32)
    pltpu.make_async_copy(esend.at[0, own], lr.at[q, r], e_recv).start()

    pa_copies = []
    for dq in range(1, LINE):
        qq = lax.rem(q + dq, LINE)
        copy = remote(
            pa.at[pl.ds(qq * OWN, OWN)], a2.at[q], pa_send.at[dq - 1], pa_recv.at[dq - 1], r, qq
        )
        copy.start()
        pa_copies.append(copy)
    pa_local = pltpu.make_async_copy(pa.at[pl.ds(q * OWN, OWN)], a2.at[q], pa_own)
    pa_local.start()

    settle(lr, e_recv)
    right = jnp.concatenate([lr[k, :, 16:32, :].reshape(TOK, COLS) for k in range(LINE)], axis=1)
    for half in range(2):
        left = jnp.concatenate(
            [lr[k, half * 16 : half * 16 + 16, 0:16, :].reshape(256, COLS) for k in range(LINE)],
            axis=1,
        )
        tri = dot(left, right, NT)
        for jb in range(LINE):
            tst[pl.ds(half * 1024 + jb, 256, stride=4), :] = tri[:, jb * 128 : jb * 128 + 128]

    @pl.loop(0, 4)
    def _(part):
        rows = pl.ds(pl.multiple_of(part * 512, 512), 512)
        tsend[rows, :] = tst[rows, :].astype(BF16)

    for offset in FAR_FIRST:
        rr, qq = peer(offset)
        rows = pl.ds(pl.multiple_of((rr * LINE + qq) * 16, 16), 16)
        remote(tsend.at[rows], trecv.at[me], t_send, t_recv, rr, qq).start()

    own = pl.ds(pl.multiple_of(me * 16, 16), 16)
    pltpu.make_async_copy(tsend.at[own], trecv.at[me], t_recv).start()

    pa_local.wait()
    for copy in pa_copies:
        copy.wait()

    @pl.loop(0, OWN)
    def _(il):
        x = a2[:, il].reshape(TOK, CH).astype(F32)
        gbuf[il] = sigmoid(dot(layer_norm(x).astype(BF16), tg[...]))

    settle(trecv, t_recv)

    def add(part, total):
        return total + jnp.sum(trecv[pl.ds(part * 16, 16)].astype(F32), axis=0)

    mean = lax.fori_loop(0, 8, add, jnp.zeros((16, 128), F32)) * (1.0 / CH)

    def add_square(part, total):
        centre = trecv[pl.ds(part * 16, 16)].astype(F32) - mean[None]
        return total + jnp.sum(centre * centre, axis=0)

    spread = lax.fori_loop(0, 8, add_square, jnp.zeros((16, 128), F32)) * (1.0 / CH)
    gain = lax.rsqrt(spread + EPS)

    @pl.loop(0, 8)
    def _(part):
        block = (trecv[pl.ds(part * 16, 16)].astype(F32) - mean[None]) * gain[None]
        for n in range(16):
            tn[pl.ds(part * 320 + n * 20, 16), :] = block[n]

    spot = lax.broadcasted_iota(jnp.int32, (16, HEADS), 0) % HEADS
    pick = (spot == lax.broadcasted_iota(jnp.int32, (16, HEADS), 1)).astype(BF16)
    bias_w = dot(pick, bp[...]).astype(BF16)
    bias_row = lax.broadcasted_iota(jnp.int32, (16, TOK), 0) // HEADS

    def update(il, own_bias):
        blocks = [
            tn[pl.ds(il * LINE + jb, 128, stride=20), :].T.astype(BF16) for jb in range(LINE)
        ]
        product = dot(jnp.concatenate(blocks, axis=0), to[...])
        x = a2[:, il].reshape(TOK, CH).astype(F32)
        updated = (x + gbuf[il] * product).astype(BF16)
        upd[core * OWN + il] = updated.reshape(16, 2, 16, CH)
        normed = layer_norm(updated.astype(F32)).astype(BF16)
        an[il] = normed.reshape(16, 2, 16, CH)
        return jnp.where(bias_row == il, dot(bias_w, normed, NT), own_bias)

    own_bias = lax.fori_loop(0, OWN, update, jnp.zeros((16, TOK), F32)).astype(BF16)
    ba[z, y, q, 0:16, :] = own_bias[:, 0:128]
    ba[z, y, q, 16:32, :] = own_bias[:, 128:256]
    bb[y, q, z] = own_bias[:, 256:384]
    bc[q, z, y] = own_bias[:, 384:512]

    parts = [(ba, "zyx"), (bb, "yxz"), (bc, "xzy")]
    at = {"z": zs, "y": ys, "x": xs}

    def spread(stage):
        copies = []
        for n, (ref, axes) in enumerate(parts):
            slot = ref.at[tuple(at[axis][0] for axis in axes[: 3 - stage])]
            for d in range(1, LINE):
                offset = {"z": 0, "y": 0, "x": 0}
                offset[axes[2 - stage]] = d
                rr, qq = peer((offset["z"], offset["y"], 0, offset["x"]))
                sem = stage * 9 + n * 3 + d - 1
                copies.append(remote(slot, slot, b_send.at[sem], b_recv.at[sem], rr, qq))
        for copy in copies:
            copy.start()
        return copies

    def spread_wait(stage):
        for n, (ref, axes) in enumerate(parts):
            for d in range(1, LINE):
                place_of = [at[axis][0] for axis in axes[: 3 - stage]]
                place_of[-1] = at[axes[2 - stage]][LINE - d]
                settle(ref.at[tuple(place_of)], b_recv.at[stage * 9 + n * 3 + d - 1])

    copies = spread(0)
    twin = place(z, y, 1 - core)
    mine = pl.ds(core * OWN, OWN)
    theirs = pl.ds((1 - core) * OWN, OWN)
    swap = remote(upd.at[mine], upd.at[mine], u_send, u_recv, twin, q)
    swap.start()

    head_of = lax.broadcasted_iota(jnp.int32, (256, CH), 1) // HEAD

    def project(n, il):
        half = an[il, :, core].reshape(256, CH)
        qs[n] = (dot(half, ap[:, 0:CH]) * (HEAD**-0.5 * LOG2E)).astype(BF16)
        gs[n] = sigmoid(dot(half, ap[:, 3 * CH : 4 * CH]))
        mixed = dot(an[il].reshape(TOK, CH), ap[:, CH : 3 * CH])
        ks[n] = mixed[:, 0:CH].astype(BF16)
        vs[n, :, 0:CH] = mixed[:, CH : 2 * CH].astype(BF16)
        vs[n, :, CH : 2 * CH] = jnp.ones((TOK, CH), BF16)

    def score(n):
        query = qs[n]
        for pair in range(2):
            masked = [
                jnp.where(head_of == pair * 2 + h, query, jnp.zeros_like(query)) for h in range(2)
            ]
            sbuf[n, pair * 512 : pair * 512 + 512, :] = dot(jnp.concatenate(masked, axis=0), ks[n], NT)

    @pl.loop(0, OWN)
    def _(il):
        project(il, il)

    score(0)
    spread_wait(0)
    copies += spread(1)

    @pl.loop(1, OWN)
    def _(n):
        score(n)

    spread_wait(1)
    copies += spread(2)
    swap.wait_recv()

    @pl.loop(0, OWN)
    def _(il):
        normed = layer_norm(upd[(1 - core) * OWN + il].reshape(TOK, CH).astype(F32)).astype(BF16)
        an[il] = normed.reshape(16, 2, 16, CH)
        project(OWN + il, il)

    @pl.loop(OWN, 2 * OWN)
    def _(n):
        score(n)

    spread_wait(2)
    key_lane = lax.broadcasted_iota(jnp.int32, (1, TOK), 1)
    key_term = jnp.where(key_lane < count, 0.0, -1e9 * LOG2E)

    @pl.loop(0, LINE)
    def _(zz):
        for yy in range(LINE):
            for xx in range(LINE):
                rows = pl.ds(pl.multiple_of(zz * 256 + yy * 64 + xx * 16, 16), 16)
                tiles = [ba[zz, yy, xx, 0:16], ba[zz, yy, xx, 16:32], bb[yy, xx, zz], bc[xx, zz, yy]]
                for kb, tile in enumerate(tiles):
                    cols = slice(kb * 128, kb * 128 + 128)
                    bias[kb, rows, :] = tile.astype(F32) * LOG2E + key_term[:, cols]

    def attend(n, own_row):
        weights = []
        for h in range(HEADS):
            for part in range(4):
                rows = slice(h * 256 + part * 64, h * 256 + part * 64 + 64)
                own = [bias[kb, pl.ds(part * 256 + h, 64, stride=4), :] for kb in range(LINE)]
                logits = sbuf[n, rows, :] + jnp.concatenate(own, axis=1)
                powers = jnp.exp2(logits - jnp.max(logits, axis=-1, keepdims=True))
                weights.append(powers.astype(BF16))
        mixed = dot(jnp.concatenate(weights, axis=0), vs[n])
        total = mixed[0:256]
        for h in range(1, HEADS):
            mask = jnp.concatenate([head_of, head_of], axis=1) == h
            total = jnp.where(mask, mixed[h * 256 : h * 256 + 256], total)
        attended = total[:, 0:CH] / total[:, CH : 2 * CH]
        gated = (attended * gs[n]).astype(BF16)
        before = upd[own_row, :, core].reshape(256, CH).astype(F32)
        result = before + dot(gated, ao[...])
        osend[n] = result.astype(BF16).reshape(LINE, 4, 16, CH)

    @pl.loop(0, OWN)
    def _(il):
        attend(OWN + il, (1 - core) * OWN + il)
        for d in range(LINE):
            jb = xs[d]
            target = out.at[q * OWN + il, :, core]
            remote(osend.at[OWN + il, jb], target, o_send, o_recv, twin, jb).start()

    @pl.loop(0, OWN)
    def _(il):
        attend(il, core * OWN + il)
        target = out.at[q * OWN + il, :, core]
        for d in range(1, LINE):
            jb = xs[d]
            remote(osend.at[il, jb], target, o_send, o_recv, r, jb).start()
        pltpu.make_async_copy(osend.at[il, q], target, o_recv).start()

    settle(out, o_recv)
    settle(osend.at[0:7], o_send)
    settle(esend.at[0:3], e_send)
    settle(esend.at[0, 0 : 31 * 32], e_send)
    settle(tsend.at[0 : 16 * (DEVICES - 1)], t_send)
    swap.wait_send()
    for copy in copies:
        copy.wait_send()


def local(pair_act, valid_count, edge_proj, edge_gate, tri_gate, tri_out, attn_proj, bias_proj, attn_out):
    hbm = pl.BlockSpec(memory_space=pltpu.HBM)
    dma = pltpu.SemaphoreType.DMA
    return pl.pallas_call(
        kernel,
        out_shape=jax.ShapeDtypeStruct((ROWS, 4, 2, 16, CH), BF16),
        in_specs=[pl.BlockSpec(memory_space=pltpu.SMEM)] + [hbm] * 8,
        out_specs=pl.BlockSpec(memory_space=pl.ANY),
        scratch_shapes=[
            pltpu.VMEM((ROWS, COLS, CH), BF16),
            pltpu.VMEM((CH, 2 * CH), BF16),
            pltpu.VMEM((CH, 2 * CH), BF16),
            pltpu.VMEM((CH, CH), BF16),
            pltpu.VMEM((CH, CH), BF16),
            pltpu.VMEM((CH, 4 * CH), BF16),
            pltpu.VMEM((HEADS, CH), BF16),
            pltpu.VMEM((CH, CH), BF16),
            pltpu.VMEM((4, 128, CH), BF16),
            pltpu.VMEM((2048, CH), BF16),
            pltpu.VMEM((32 * 36, COLS), F32),
            pltpu.VMEM((4, 1024, COLS), BF16),
            pltpu.VMEM((LINE, 32, 32, COLS), BF16),
            pltpu.VMEM((2048, 128), F32),
            pltpu.VMEM((2048, 128), BF16),
            pltpu.VMEM((CH, 16, 128), BF16),
            pltpu.VMEM((CH * 20, 128), F32),
            pltpu.VMEM((OWN, TOK, CH), F32),
            pltpu.VMEM((LINE, OWN, COLS, CH), BF16),
            pltpu.VMEM((2 * OWN, 16, 2, 16, CH), BF16),
            pltpu.VMEM((OWN, 16, 2, 16, CH), BF16),
            pltpu.VMEM((2 * OWN, 256, CH), BF16),
            pltpu.VMEM((2 * OWN, TOK, CH), BF16),
            pltpu.VMEM((2 * OWN, TOK, 2 * CH), BF16),
            pltpu.VMEM((2 * OWN, 256, CH), F32),
            pltpu.VMEM((LINE, LINE, LINE, 32, 128), BF16),
            pltpu.VMEM((LINE, LINE, LINE, 16, 128), BF16),
            pltpu.VMEM((LINE, LINE, LINE, 16, 128), BF16),
            pltpu.VMEM((2 * OWN, 1024, TOK), F32),
            pltpu.VMEM((LINE, 1024, 128), F32),
            pltpu.VMEM((2 * OWN, LINE, 4, 16, CH), BF16),
            pltpu.SemaphoreType.REGULAR, dma((8,)), dma((3,)), dma((3,)), dma, dma, dma, dma, dma,
            dma((27,)), dma((27,)), dma, dma, dma, dma,
        ],
        compiler_params=pltpu.CompilerParams(
            collective_id=0, has_side_effects=True, vmem_limit_bytes=63 * 1024 * 1024
        ),
        name="triangle",
    )(valid_count, pair_act, edge_proj, edge_gate, tri_gate, tri_out, attn_proj, bias_proj.T, attn_out).reshape(ROWS, COLS, CH)


def solution(mesh):
    placed = (P("row", "ch", None), P(), P(), P(), P(), P(), P(), P(), P())
    return jax.shard_map(
        local, mesh=mesh, in_specs=placed, out_specs=P("row", "ch", None), check_vma=False
    )
```

```python
import math

import jax
import jax.numpy as jnp
from jax import lax
from jax.experimental import pallas as pl
from jax.experimental.pallas import tpu as pltpu
from jax.sharding import PartitionSpec as P

MESH = pl.DeviceIdType.MESH
EPS = 1e-05
F32 = jnp.float32
BF16 = jnp.bfloat16
LOG2E = math.log2(math.e)
NT = (((1,), (1,)), ((), ()))
NN = (((1,), (0,)), ((), ()))

LINE = 4
ROWS = 16
COLS = 128
CH = 128
TOK = 512
HEADS = 4
HEAD = 32
OWN = 4
DEVICES = 128


OFFSETS = [
    (dz, dy, dc, dx) for dz in range(LINE) for dy in range(LINE) for dc in range(2) for dx in range(LINE)
][1:]


def hops(offset):
    dz, dy, _, dx = offset
    return sum(min(d, LINE - d) for d in (dz, dy, dx))


FAR_FIRST = sorted(OFFSETS, key=hops, reverse=True)


def dot(a, b, dims=NN):
    return lax.dot_general(a, b, dims, preferred_element_type=F32)


def sigmoid(x):
    return 0.5 * jnp.tanh(0.5 * x) + 0.5


def layer_norm(x):
    centre = x - jnp.mean(x, axis=-1, keepdims=True)
    spread = jnp.mean(centre * centre, axis=-1, keepdims=True)
    return centre * lax.rsqrt(spread + EPS)


def kernel(
    count_ref, pa_in, ep_in, eg_in, tg_in, to_in, ap_in, bp_in, ao_in,
    out,
    pa, ep, eg, tg, to, ap, bp, ao, wt, nrm, ebuf, esend, lr, tst, tsend, trecv, tn, gbuf, a2, upd, an, qs, ks, vs, gs, ba, bb, bc, sbuf, bias, osend,
    ready, load, pa_send, pa_recv, pa_own, e_send, e_recv, t_send, t_recv,
    p_send, p_recv, l_send, l_recv, u_send, u_recv, o_send, o_recv,
):
    r = lax.axis_index("row")
    q = lax.axis_index("ch")
    me = r * LINE + q
    z = lax.div(r, 8)
    y = lax.rem(lax.div(r, 2), 4)
    core = lax.rem(r, 2)
    count = count_ref[0]

    def place(zz, yy, cc):
        return zz * 8 + yy * 2 + cc

    zs = [lax.rem(z + d, LINE) for d in range(LINE)]
    ys = [lax.rem(y + d, LINE) for d in range(LINE)]
    xs = [lax.rem(q + d, LINE) for d in range(LINE)]
    cores = [core, 1 - core]

    def peer(offset):
        dz, dy, dc, dx = offset
        return place(zs[dz], ys[dy], cores[dc]), xs[dx]

    def remote(src, dst, send, recv, rr, qq):
        return pltpu.make_async_remote_copy(
            src_ref=src, dst_ref=dst, send_sem=send, recv_sem=recv,
            device_id=(rr, qq), device_id_type=MESH,
        )

    def settle(ref, sem):
        pltpu.make_async_copy(ref, ref, sem).wait()

    loads = [
        pltpu.make_async_copy(src, dst, load.at[n])
        for n, (src, dst) in enumerate(
            [(ep_in, ep), (eg_in, eg), (pa_in, pa), (tg_in, tg), (to_in, to), (ap_in, ap), (bp_in, bp), (ao_in, ao)]
        )
    ]
    for copy in loads:
        copy.start()

    barrier = pltpu.get_barrier_semaphore()

    plane = [o for o in OFFSETS if o[2] == 0 and o[3] == 0]
    near = [o for o in OFFSETS if o[0] == 0 and o[1] == 0] + plane
    for offset in near:
        rr, qq = peer(offset)
        pl.semaphore_signal(barrier, inc=1, device_id=(rr, qq), device_id_type=MESH)

    for copy in loads:
        copy.wait()

    @pl.loop(0, 4)
    def _(part):
        x = pa[pl.ds(part * 4, 4)].reshape(512, CH).astype(F32)
        nrm[pl.ds(pl.multiple_of(part * 512, 512), 512), :] = layer_norm(x).astype(BF16)

    pl.semaphore_wait(barrier, len(near))
    for offset in plane:
        rr, qq = peer(offset)
        pl.semaphore_signal(ready, inc=1, device_id=(rr, qq), device_id_type=MESH)

    spot = lax.broadcasted_iota(jnp.int32, (CH, CH), 0)
    line = spot % 32
    chosen = line * 4 + (spot // 32 + 8 - line // 8 - (line // 2) % 4) % 4
    order = (chosen == lax.broadcasted_iota(jnp.int32, (CH, CH), 1)).astype(BF16)
    for n, ref in enumerate((ep, ep, eg, eg)):
        side = n % 2
        part = dot(order, ref[:, side * CH : side * CH + CH], NT).astype(BF16)
        for m in range(4):
            wt[m, n * 32 : n * 32 + 32, :] = part[m * 32 : m * 32 + 32]
    lane = lax.broadcasted_iota(jnp.int32, (1, 512), 1)

    def edges_of(k):
        weights = wt[lax.rem(z + y + q + k, 4)]
        for part in range(4):
            both = dot(weights, nrm[part * 512 : part * 512 + 512, :], NT)
            row_token = r * ROWS + part * 4 + lane // 128
            col_token = q * COLS + lane % 128
            valid = jnp.where((row_token < count) & (col_token < count), 1.0, 0.0)
            edges = sigmoid(both[64:128]) * both[0:64] * valid
            for i in range(4):
                for side in range(2):
                    ebuf[pl.ds(side * 16 + part * 4 + i, 32, stride=36), :] = edges[
                        side * 32 : side * 32 + 32, i * 128 : i * 128 + 128
                    ]
        for n in range(32):
            esend[k, n * 32 : n * 32 + 32, :] = ebuf[n * 36 : n * 36 + 32, :].astype(BF16)

    for step, k in enumerate((2, 1, 3, 0)):
        edges_of(k)
        if step == 0:
            pl.semaphore_wait(ready, len(plane))
        for offset in FAR_FIRST:
            if (offset[0] + offset[1] + offset[3]) % 4 == k:
                rr, qq = peer(offset)
                rows = pl.ds(pl.multiple_of(rr * 32, 32), 32)
                remote(esend.at[k, rows], lr.at[q, z * LINE + y, core], e_send, e_recv, rr, qq).start()

    own = pl.ds(pl.multiple_of(r * 32, 32), 32)
    pltpu.make_async_copy(esend.at[0, own], lr.at[q, z * LINE + y, core], e_recv).start()

    pa_copies = []
    for dq in range(1, LINE):
        qq = lax.rem(q + dq, LINE)
        copy = remote(
            pa.at[pl.ds(qq * OWN, OWN)], a2.at[q], pa_send.at[dq - 1], pa_recv.at[dq - 1], r, qq
        )
        copy.start()
        pa_copies.append(copy)
    pa_local = pltpu.make_async_copy(pa.at[pl.ds(q * OWN, OWN)], a2.at[q], pa_own)
    pa_local.start()

    settle(lr, e_recv)
    right = jnp.concatenate([lr[k, :, :, 16:32, :].reshape(TOK, COLS) for k in range(LINE)], axis=1)
    for dc in (1, 0):
        left = jnp.concatenate(
            [lr[k, :, cores[dc], 0:16, :].reshape(256, COLS) for k in range(LINE)], axis=1
        )
        tri = dot(left, right, NT)
        for jb in range(LINE):
            tst[dc, pl.ds(jb, 256, stride=4), :] = tri[:, jb * 128 : jb * 128 + 128]
        tsend[dc] = tst[dc].astype(BF16)
        for offset in FAR_FIRST:
            if offset[2] == dc:
                rr, qq = peer(offset)
                rows = pl.ds(pl.multiple_of((zs[offset[0]] * 16 + ys[offset[1]] * 4 + qq) * 16, 16), 16)
                remote(tsend.at[dc, rows], trecv.at[me], t_send, t_recv, rr, qq).start()

    own = pl.ds(pl.multiple_of((z * 16 + y * 4 + q) * 16, 16), 16)
    pltpu.make_async_copy(tsend.at[0, own], trecv.at[me], t_recv).start()

    pa_local.wait()
    for copy in pa_copies:
        copy.wait()

    @pl.loop(0, OWN)
    def _(jb):
        x = a2[jb].reshape(TOK, CH).astype(F32)
        gbuf[jb] = sigmoid(dot(layer_norm(x).astype(BF16), tg[...]))

    settle(trecv, t_recv)

    def add(part, total):
        return total + jnp.sum(trecv[pl.ds(part * 16, 16)].astype(F32), axis=0)

    mean = lax.fori_loop(0, 8, add, jnp.zeros((16, 128), F32)) * (1.0 / CH)

    def add_square(part, total):
        centre = trecv[pl.ds(part * 16, 16)].astype(F32) - mean[None]
        return total + jnp.sum(centre * centre, axis=0)

    spread = lax.fori_loop(0, 8, add_square, jnp.zeros((16, 128), F32)) * (1.0 / CH)
    gain = lax.rsqrt(spread + EPS)

    @pl.loop(0, 8)
    def _(part):
        block = (trecv[pl.ds(part * 16, 16)].astype(F32) - mean[None]) * gain[None]
        for n in range(16):
            tn[pl.ds(part * 320 + n * 20, 16), :] = block[n]

    spot = lax.broadcasted_iota(jnp.int32, (16, HEADS), 0) % HEADS
    pick = (spot == lax.broadcasted_iota(jnp.int32, (16, HEADS), 1)).astype(BF16)
    bias_w = dot(pick, bp[...]).astype(BF16)
    bias_row = lax.broadcasted_iota(jnp.int32, (16, 128), 0) // HEADS

    u = z + core * (y - z)
    v = y + core * (z - y)
    us = [lax.rem(u + d, LINE) for d in range(LINE)]
    vvs = [lax.rem(v + d, LINE) for d in range(LINE)]
    step_u = 8 - 6 * core
    step_v = 2 + 6 * core
    parts = [(ba, us, vvs, xs), (bb, vvs, us, xs), (bc, xs, us, vvs)]

    def at(n, line, first, second):
        uu, vv, xx = [
            (us[line], vvs[first], xs[second]),
            (us[first], vvs[line], xs[second]),
            (us[first], vvs[second], xs[line]),
        ][n]
        return uu * step_u + vv * step_v + core, xx

    def over_plane(n):
        ref, lines, firsts, seconds = parts[n]
        slot = ref.at[lines[0], firsts[0] * LINE + seconds[0]]
        pairs = [(f, t) for f in range(LINE) for t in range(LINE)][1:]
        for f, t in sorted(pairs, key=lambda p: -min(p[0], LINE - p[0]) - min(p[1], LINE - p[1])):
            remote(slot, slot, p_send.at[n], p_recv.at[n], *at(n, 0, f, t)).start()

    def along_line(n):
        ref, lines, _, _ = parts[n]
        settle(ref.at[lines[0], 0:15], p_recv.at[n])
        for d in (2, 1, 3):
            slot = ref.at[lines[0]]
            remote(slot, slot, l_send.at[n], l_recv.at[n], *at(n, d, 0, 0)).start()

    mine = pl.ds(core * OWN, OWN)
    for jb in range(LINE):
        blocks = [
            tn[pl.ds(il * LINE + jb, 128, stride=20), :].T.astype(BF16) for il in range(OWN)
        ]
        product = dot(jnp.concatenate(blocks, axis=0), to[...])
        x = a2[jb].reshape(TOK, CH).astype(F32)
        updated = (x + gbuf[jb] * product).astype(BF16)
        upd[mine, jb * 4 : jb * 4 + 4] = updated.reshape(OWN, 4, 2, 16, CH)
        normed = layer_norm(updated.astype(F32)).astype(BF16)
        an[:, jb * 4 : jb * 4 + 4] = normed.reshape(OWN, 4, 2, 16, CH)
        biases = dot(bias_w, normed, NT)
        tile = biases[:, 0:128]
        for il in range(1, OWN):
            tile = jnp.where(bias_row == il, biases[:, il * 128 : il * 128 + 128], tile)
        tile = tile.astype(BF16)
        if jb < 2:
            ba[u, v * LINE + q, jb * 16 : jb * 16 + 16, :] = tile
        elif jb == 2:
            bb[v, u * LINE + q] = tile
        else:
            bc[q, u * LINE + v] = tile
        if jb > 0:
            over_plane(jb - 1)

    twin = place(z, y, 1 - core)
    swap = remote(upd.at[mine], upd.at[mine], u_send, u_recv, twin, q)
    swap.start()

    head_of = lax.broadcasted_iota(jnp.int32, (256, CH), 1) // HEAD

    def project(n, il):
        half = an[il, :, core].reshape(256, CH)
        qs[n] = (dot(half, ap[:, 0:CH]) * (HEAD**-0.5 * LOG2E)).astype(BF16)
        gs[n] = sigmoid(dot(half, ap[:, 3 * CH : 4 * CH]))
        mixed = dot(an[il].reshape(TOK, CH), ap[:, CH : 3 * CH])
        ks[n] = mixed[:, 0:CH].astype(BF16)
        vs[n, :, 0:CH] = mixed[:, CH : 2 * CH].astype(BF16)
        vs[n, :, CH : 2 * CH] = jnp.ones((TOK, CH), BF16)

    def score(n):
        query = qs[n]
        for pair in range(2):
            masked = [
                jnp.where(head_of == pair * 2 + h, query, jnp.zeros_like(query)) for h in range(2)
            ]
            sbuf[n, pair * 512 : pair * 512 + 512, :] = dot(jnp.concatenate(masked, axis=0), ks[n], NT)

    @pl.loop(0, OWN)
    def _(il):
        project(il, il)

    score(0)
    along_line(0)
    score(1)
    along_line(1)
    along_line(2)

    @pl.loop(2, OWN)
    def _(n):
        score(n)

    swap.wait_recv()

    @pl.loop(0, OWN)
    def _(il):
        normed = layer_norm(upd[(1 - core) * OWN + il].reshape(TOK, CH).astype(F32)).astype(BF16)
        an[il] = normed.reshape(16, 2, 16, CH)
        project(OWN + il, il)

    @pl.loop(OWN, 2 * OWN)
    def _(n):
        score(n)

    for n, (ref, _, _, _) in enumerate(parts):
        settle(ref.at[0:3], l_recv.at[n])
    key_lane = lax.broadcasted_iota(jnp.int32, (1, TOK), 1)
    key_term = jnp.where(key_lane < count, 0.0, -1e9 * LOG2E)
    rows_u = 256 - 192 * core
    rows_v = 64 + 192 * core

    @pl.loop(0, LINE)
    def _(uu):
        for vv in range(LINE):
            for xx in range(LINE):
                rows = pl.ds(pl.multiple_of(uu * rows_u + vv * rows_v + xx * 16, 16), 16)
                pair = ba[uu, vv * LINE + xx]
                tiles = [pair[0:16], pair[16:32], bb[vv, uu * LINE + xx], bc[xx, uu * LINE + vv]]
                for kb, tile in enumerate(tiles):
                    cols = slice(kb * 128, kb * 128 + 128)
                    bias[kb, rows, :] = tile.astype(F32) * LOG2E + key_term[:, cols]

    @pl.loop(0, 2 * OWN)
    def _(n):
        weights = []
        for h in range(HEADS):
            for part in range(4):
                rows = slice(h * 256 + part * 64, h * 256 + part * 64 + 64)
                own = [bias[kb, pl.ds(part * 256 + h, 64, stride=4), :] for kb in range(LINE)]
                logits = sbuf[n, rows, :] + jnp.concatenate(own, axis=1)
                powers = jnp.exp2(logits - jnp.max(logits, axis=-1, keepdims=True))
                weights.append(powers.astype(BF16))
        mixed = dot(jnp.concatenate(weights, axis=0), vs[n])
        total = mixed[0:256]
        for h in range(1, HEADS):
            mask = jnp.concatenate([head_of, head_of], axis=1) == h
            total = jnp.where(mask, mixed[h * 256 : h * 256 + 256], total)
        attended = total[:, 0:CH] / total[:, CH : 2 * CH]
        gated = (attended * gs[n]).astype(BF16)
        owner = core + (1 - 2 * core) * (n // OWN)
        before = upd[owner * OWN + n % OWN, :, core].reshape(256, CH).astype(F32)
        result = before + dot(gated, ao[...])
        osend[n] = result.astype(BF16).reshape(LINE, 4, 16, CH)
        target = out.at[q * OWN + n % OWN, :, core]
        for d in (2, 1, 3):
            remote(osend.at[n, xs[d]], target, o_send, o_recv, place(z, y, owner), xs[d]).start()

    target = out.at[pl.ds(q * OWN, OWN), :, core]
    remote(osend.at[OWN : 2 * OWN, q], target, o_send, o_recv, twin, q).start()
    pltpu.make_async_copy(osend.at[0:OWN, q], target, o_recv).start()

    settle(out, o_recv)
    settle(osend.at[0:7], o_send)
    settle(esend.at[0:3], e_send)
    settle(esend.at[0, 0 : 31 * 32], e_send)
    settle(tsend.at[1], t_send)
    settle(tsend.at[0, 0 : 63 * 16], t_send)
    swap.wait_send()
    for n, (ref, _, _, _) in enumerate(parts):
        settle(ref.at[0, 0:15], p_send.at[n])
        settle(ref.at[0:3], l_send.at[n])


def local(pair_act, valid_count, edge_proj, edge_gate, tri_gate, tri_out, attn_proj, bias_proj, attn_out):
    hbm = pl.BlockSpec(memory_space=pltpu.HBM)
    dma = pltpu.SemaphoreType.DMA
    return pl.pallas_call(
        kernel,
        out_shape=jax.ShapeDtypeStruct((ROWS, 4, 2, 16, CH), BF16),
        in_specs=[pl.BlockSpec(memory_space=pltpu.SMEM)] + [hbm] * 8,
        out_specs=pl.BlockSpec(memory_space=pl.ANY),
        scratch_shapes=[
            pltpu.VMEM((ROWS, COLS, CH), BF16),
            pltpu.VMEM((CH, 2 * CH), BF16),
            pltpu.VMEM((CH, 2 * CH), BF16),
            pltpu.VMEM((CH, CH), BF16),
            pltpu.VMEM((CH, CH), BF16),
            pltpu.VMEM((CH, 4 * CH), BF16),
            pltpu.VMEM((HEADS, CH), BF16),
            pltpu.VMEM((CH, CH), BF16),
            pltpu.VMEM((4, 128, CH), BF16),
            pltpu.VMEM((2048, CH), BF16),
            pltpu.VMEM((32 * 36, COLS), F32),
            pltpu.VMEM((4, 1024, COLS), BF16),
            pltpu.VMEM((LINE, 16, 2, 32, COLS), BF16),
            pltpu.VMEM((2, 1024, 128), F32),
            pltpu.VMEM((2, 1024, 128), BF16),
            pltpu.VMEM((CH, 16, 128), BF16),
            pltpu.VMEM((CH * 20, 128), F32),
            pltpu.VMEM((OWN, TOK, CH), F32),
            pltpu.VMEM((LINE, OWN, COLS, CH), BF16),
            pltpu.VMEM((2 * OWN, 16, 2, 16, CH), BF16),
            pltpu.VMEM((OWN, 16, 2, 16, CH), BF16),
            pltpu.VMEM((2 * OWN, 256, CH), BF16),
            pltpu.VMEM((2 * OWN, TOK, CH), BF16),
            pltpu.VMEM((2 * OWN, TOK, 2 * CH), BF16),
            pltpu.VMEM((2 * OWN, 256, CH), F32),
            pltpu.VMEM((LINE, 16, 32, 128), BF16),
            pltpu.VMEM((LINE, 16, 16, 128), BF16),
            pltpu.VMEM((LINE, 16, 16, 128), BF16),
            pltpu.VMEM((2 * OWN, 1024, TOK), F32),
            pltpu.VMEM((LINE, 1024, 128), F32),
            pltpu.VMEM((2 * OWN, LINE, 4, 16, CH), BF16),
            pltpu.SemaphoreType.REGULAR, dma((8,)), dma((3,)), dma((3,)), dma, dma, dma, dma, dma,
            dma((3,)), dma((3,)), dma((3,)), dma((3,)), dma, dma, dma, dma,
        ],
        compiler_params=pltpu.CompilerParams(
            collective_id=0, has_side_effects=True, vmem_limit_bytes=63 * 1024 * 1024
        ),
        name="triangle",
    )(valid_count, pair_act, edge_proj, edge_gate, tri_gate, tri_out, attn_proj, bias_proj.T, attn_out).reshape(ROWS, COLS, CH)


def solution(mesh):
    placed = (P("row", "ch", None), P(), P(), P(), P(), P(), P(), P(), P())
    return jax.shard_map(
        local, mesh=mesh, in_specs=placed, out_specs=P("row", "ch", None), check_vma=False
    )
```

```python
import math

import jax
import jax.numpy as jnp
from jax import lax
from jax.experimental import pallas as pl
from jax.experimental.pallas import tpu as pltpu
from jax.sharding import PartitionSpec as P

MESH = pl.DeviceIdType.MESH
EPS = 1e-05
F32 = jnp.float32
BF16 = jnp.bfloat16
LOG2E = math.log2(math.e)
NT = (((1,), (1,)), ((), ()))
NN = (((1,), (0,)), ((), ()))

LINE = 4
ROWS = 16
COLS = 128
CH = 128
TOK = 512
HEADS = 4
HEAD = 32
OWN = 4
DEVICES = 128


OFFSETS = [
    (dz, dy, dc, dx) for dz in range(LINE) for dy in range(LINE) for dc in range(2) for dx in range(LINE)
][1:]


def hops(offset):
    dz, dy, _, dx = offset
    return sum(min(d, LINE - d) for d in (dz, dy, dx))


FAR_FIRST = sorted(OFFSETS, key=hops, reverse=True)


def dot(a, b, dims=NN):
    return lax.dot_general(a, b, dims, preferred_element_type=F32)


def sigmoid(x):
    return 0.5 * jnp.tanh(0.5 * x) + 0.5


def layer_norm(x):
    centre = x - jnp.mean(x, axis=-1, keepdims=True)
    spread = jnp.mean(centre * centre, axis=-1, keepdims=True)
    return centre * lax.rsqrt(spread + EPS)


def kernel(
    count_ref, pa_in, ep_in, eg_in, tg_in, to_in, ap_in, bp_in, ao_in,
    out,
    pa, ep, eg, tg, to, ap, bp, ao, wt, nrm, ebuf, esend, lr, tst, tsend, trecv, tn, gbuf, a2, upd, an, qs, ks, vs, gs, ba, bb, bc, sbuf, raw, bias, osend,
    ready, load, pa_send, pa_recv, pa_own, e_send, e_recv, t_send, t_recv,
    p_send, p_recv, l_send, l_recv, u_send, u_recv, o_send, o_recv,
):
    r = lax.axis_index("row")
    q = lax.axis_index("ch")
    me = r * LINE + q
    z = lax.div(r, 8)
    y = lax.rem(lax.div(r, 2), 4)
    core = lax.rem(r, 2)
    count = count_ref[0]

    def place(zz, yy, cc):
        return zz * 8 + yy * 2 + cc

    zs = [lax.rem(z + d, LINE) for d in range(LINE)]
    ys = [lax.rem(y + d, LINE) for d in range(LINE)]
    xs = [lax.rem(q + d, LINE) for d in range(LINE)]
    cores = [core, 1 - core]

    def peer(offset):
        dz, dy, dc, dx = offset
        return place(zs[dz], ys[dy], cores[dc]), xs[dx]

    def remote(src, dst, send, recv, rr, qq):
        return pltpu.make_async_remote_copy(
            src_ref=src, dst_ref=dst, send_sem=send, recv_sem=recv,
            device_id=(rr, qq), device_id_type=MESH,
        )

    def settle(ref, sem):
        pltpu.make_async_copy(ref, ref, sem).wait()

    loads = [
        pltpu.make_async_copy(src, dst, load.at[n])
        for n, (src, dst) in enumerate(
            [(ep_in, ep), (eg_in, eg), (pa_in, pa), (tg_in, tg), (to_in, to), (ap_in, ap), (bp_in, bp), (ao_in, ao)]
        )
    ]
    for copy in loads:
        copy.start()

    barrier = pltpu.get_barrier_semaphore()

    plane = [o for o in OFFSETS if o[2] == 0 and o[3] == 0]
    near = [o for o in OFFSETS if o[0] == 0 and o[1] == 0] + plane
    for offset in near:
        rr, qq = peer(offset)
        pl.semaphore_signal(barrier, inc=1, device_id=(rr, qq), device_id_type=MESH)

    for copy in loads:
        copy.wait()

    @pl.loop(0, 4)
    def _(part):
        x = pa[pl.ds(part * 4, 4)].reshape(512, CH).astype(F32)
        nrm[pl.ds(pl.multiple_of(part * 512, 512), 512), :] = layer_norm(x).astype(BF16)

    pl.semaphore_wait(barrier, len(near))
    for offset in plane:
        rr, qq = peer(offset)
        pl.semaphore_signal(ready, inc=1, device_id=(rr, qq), device_id_type=MESH)

    spot = lax.broadcasted_iota(jnp.int32, (CH, CH), 0)
    line = spot % 32
    chosen = line * 4 + (spot // 32 + 8 - line // 8 - (line // 2) % 4) % 4
    order = (chosen == lax.broadcasted_iota(jnp.int32, (CH, CH), 1)).astype(BF16)
    for n, ref in enumerate((ep, ep, eg, eg)):
        side = n % 2
        part = dot(order, ref[:, side * CH : side * CH + CH], NT).astype(BF16)
        for m in range(4):
            wt[m, n * 32 : n * 32 + 32, :] = part[m * 32 : m * 32 + 32]
    lane = lax.broadcasted_iota(jnp.int32, (1, 512), 1)

    def edges_of(k):
        weights = wt[lax.rem(z + y + q + k, 4)]
        for part in range(4):
            both = dot(weights, nrm[part * 512 : part * 512 + 512, :], NT)
            row_token = r * ROWS + part * 4 + lane // 128
            col_token = q * COLS + lane % 128
            valid = jnp.where((row_token < count) & (col_token < count), 1.0, 0.0)
            edges = sigmoid(both[64:128]) * both[0:64] * valid
            for i in range(4):
                for side in range(2):
                    ebuf[pl.ds(side * 16 + part * 4 + i, 32, stride=36), :] = edges[
                        side * 32 : side * 32 + 32, i * 128 : i * 128 + 128
                    ]
        for n in range(32):
            esend[k, n * 32 : n * 32 + 32, :] = ebuf[n * 36 : n * 36 + 32, :].astype(BF16)

    for step, k in enumerate((2, 1, 3, 0)):
        edges_of(k)
        if step == 0:
            pl.semaphore_wait(ready, len(plane))
        targets = [o for o in FAR_FIRST if (o[0] + o[1] + o[3]) % 4 == k]

        @pl.when(core == 0)
        def _():
            for offset in targets:
                rr, qq = peer(offset)
                rows = pl.ds(pl.multiple_of(rr * 32, 32), 32)
                remote(esend.at[k, rows], lr.at[q, z * LINE + y, 0], e_send.at[0], e_recv.at[0], rr, qq).start()

        @pl.when(core == 1)
        def _():
            for offset in targets:
                rr, qq = peer(offset)
                rows = pl.ds(pl.multiple_of(rr * 32 + 16, 16), 16)
                remote(
                    esend.at[k, rows], lr.at[q, z * LINE + y, 1, 16:32], e_send.at[1], e_recv.at[1], rr, qq
                ).start()

    @pl.when(core == 0)
    def _():
        own = pl.ds(pl.multiple_of(r * 32, 32), 32)
        pltpu.make_async_copy(esend.at[0, own], lr.at[q, z * LINE + y, 0], e_recv.at[0]).start()

    @pl.when(core == 1)
    def _():
        own = pl.ds(pl.multiple_of(r * 32 + 16, 16), 16)
        pltpu.make_async_copy(esend.at[0, own], lr.at[q, z * LINE + y, 1, 16:32], e_recv.at[1]).start()
        settle(tsend.at[0], e_send.at[1])
        settle(tsend.at[0, 0 : 63 * 16], e_send.at[1])
        for offset in FAR_FIRST:
            rr, qq = peer(offset)
            rows = pl.ds(pl.multiple_of(rr * 32, 32), 16)
            k = (offset[0] + offset[1] + offset[3]) % 4
            remote(
                esend.at[k, rows], lr.at[q, z * LINE + y, 1, 0:16], e_send.at[2], e_recv.at[2], rr, qq
            ).start()
        own = pl.ds(pl.multiple_of(r * 32, 32), 16)
        pltpu.make_async_copy(esend.at[0, own], lr.at[q, z * LINE + y, 1, 0:16], e_recv.at[2]).start()

    pa_copies = []
    for dq in range(1, LINE):
        qq = lax.rem(q + dq, LINE)
        copy = remote(
            pa.at[pl.ds(qq * OWN, OWN)], a2.at[q], pa_send.at[dq - 1], pa_recv.at[dq - 1], r, qq
        )
        copy.start()
        pa_copies.append(copy)
    pa_local = pltpu.make_async_copy(pa.at[pl.ds(q * OWN, OWN)], a2.at[q], pa_own)
    pa_local.start()

    settle(lr.at[:, :, 0], e_recv.at[0])
    settle(lr.at[:, :, 1, 16:32], e_recv.at[1])
    right = jnp.concatenate([lr[k, :, :, 16:32, :].reshape(TOK, COLS) for k in range(LINE)], axis=1)
    for half in range(2):
        if half == 1:
            settle(lr.at[:, :, 1, 0:16], e_recv.at[2])
        left = jnp.concatenate(
            [lr[k, :, half, 0:16, :].reshape(256, COLS) for k in range(LINE)], axis=1
        )
        tri = dot(left, right, NT)
        for jb in range(LINE):
            tst[half, pl.ds(jb, 256, stride=4), :] = tri[:, jb * 128 : jb * 128 + 128]
        tsend[half] = tst[half].astype(BF16)
        for offset in FAR_FIRST:
            if offset[2] == 0:
                zz, yy, qq = zs[offset[0]], ys[offset[1]], xs[offset[3]]
                rows = pl.ds(pl.multiple_of((zz * 16 + yy * 4 + qq) * 16, 16), 16)
                remote(
                    tsend.at[half, rows], trecv.at[me], t_send.at[half], t_recv, place(zz, yy, half), qq
                ).start()
        own = pl.ds(pl.multiple_of((z * 16 + y * 4 + q) * 16, 16), 16)

        @pl.when(core == half)
        def _():
            pltpu.make_async_copy(tsend.at[half, own], trecv.at[me], t_recv).start()

        @pl.when(core != half)
        def _():
            remote(
                tsend.at[half, own], trecv.at[me], t_send.at[half], t_recv, place(z, y, half), q
            ).start()

    pa_local.wait()
    for copy in pa_copies:
        copy.wait()

    @pl.loop(0, OWN)
    def _(jb):
        x = a2[jb].reshape(TOK, CH).astype(F32)
        gbuf[jb] = sigmoid(dot(layer_norm(x).astype(BF16), tg[...]))

    settle(trecv, t_recv)

    def add(part, total):
        return total + jnp.sum(trecv[pl.ds(part * 16, 16)].astype(F32), axis=0)

    mean = lax.fori_loop(0, 8, add, jnp.zeros((16, 128), F32)) * (1.0 / CH)

    def add_square(part, total):
        centre = trecv[pl.ds(part * 16, 16)].astype(F32) - mean[None]
        return total + jnp.sum(centre * centre, axis=0)

    spread = lax.fori_loop(0, 8, add_square, jnp.zeros((16, 128), F32)) * (1.0 / CH)
    gain = lax.rsqrt(spread + EPS)

    @pl.loop(0, 8)
    def _(part):
        block = (trecv[pl.ds(part * 16, 16)].astype(F32) - mean[None]) * gain[None]
        for n in range(16):
            tn[pl.ds(part * 320 + n * 20, 16), :] = block[n]

    spot = lax.broadcasted_iota(jnp.int32, (16, HEADS), 0) % HEADS
    pick = (spot == lax.broadcasted_iota(jnp.int32, (16, HEADS), 1)).astype(BF16)
    bias_w = dot(pick, bp[...]).astype(BF16)
    bias_row = lax.broadcasted_iota(jnp.int32, (16, 128), 0) // HEADS

    u = z + core * (y - z)
    v = y + core * (z - y)
    us = [lax.rem(u + d, LINE) for d in range(LINE)]
    vvs = [lax.rem(v + d, LINE) for d in range(LINE)]
    step_u = 8 - 6 * core
    step_v = 2 + 6 * core
    parts = [(ba, us, vvs, xs), (bb, vvs, us, xs), (bc, xs, us, vvs)]

    def at(n, line, first, second):
        uu, vv, xx = [
            (us[line], vvs[first], xs[second]),
            (us[first], vvs[line], xs[second]),
            (us[first], vvs[second], xs[line]),
        ][n]
        return uu * step_u + vv * step_v + core, xx

    def over_plane(n):
        ref, lines, firsts, seconds = parts[n]
        slot = ref.at[lines[0], firsts[0] * LINE + seconds[0]]
        pairs = [(f, t) for f in range(LINE) for t in range(LINE)][1:]
        for f, t in sorted(pairs, key=lambda p: -min(p[0], LINE - p[0]) - min(p[1], LINE - p[1])):
            remote(slot, slot, p_send.at[n], p_recv.at[n], *at(n, 0, f, t)).start()

    def along_line(n):
        ref, lines, _, _ = parts[n]
        settle(ref.at[lines[0], 0:15], p_recv.at[n])
        for d in (2, 1, 3):
            slot = ref.at[lines[0]]
            remote(slot, slot, l_send.at[n], l_recv.at[n], *at(n, d, 0, 0)).start()

    mine = pl.ds(core * OWN, OWN)
    for jb in range(LINE):
        blocks = [
            tn[pl.ds(il * LINE + jb, 128, stride=20), :].T.astype(BF16) for il in range(OWN)
        ]
        product = dot(jnp.concatenate(blocks, axis=0), to[...])
        x = a2[jb].reshape(TOK, CH).astype(F32)
        updated = (x + gbuf[jb] * product).astype(BF16)
        upd[mine, jb * 4 : jb * 4 + 4] = updated.reshape(OWN, 4, 2, 16, CH)
        normed = layer_norm(updated.astype(F32)).astype(BF16)
        an[:, jb * 4 : jb * 4 + 4] = normed.reshape(OWN, 4, 2, 16, CH)
        biases = dot(bias_w, normed, NT)
        tile = biases[:, 0:128]
        for il in range(1, OWN):
            tile = jnp.where(bias_row == il, biases[:, il * 128 : il * 128 + 128], tile)
        tile = tile.astype(BF16)
        if jb < 2:
            ba[u, v * LINE + q, jb * 16 : jb * 16 + 16, :] = tile
        elif jb == 2:
            bb[v, u * LINE + q] = tile
        else:
            bc[q, u * LINE + v] = tile
        if jb == 1:
            over_plane(0)
    over_plane(1)
    over_plane(2)

    twin = place(z, y, 1 - core)
    swap = remote(upd.at[mine], upd.at[mine], u_send, u_recv, twin, q)
    swap.start()

    head_of = lax.broadcasted_iota(jnp.int32, (256, CH), 1) // HEAD

    def project(n, il):
        half = an[il, :, core].reshape(256, CH)
        qs[n] = (dot(half, ap[:, 0:CH]) * (HEAD**-0.5 * LOG2E)).astype(BF16)
        gs[n] = sigmoid(dot(half, ap[:, 3 * CH : 4 * CH]))
        mixed = dot(an[il].reshape(TOK, CH), ap[:, CH : 3 * CH])
        ks[n] = mixed[:, 0:CH].astype(BF16)
        vs[n, :, 0:CH] = mixed[:, CH : 2 * CH].astype(BF16)
        vs[n, :, CH : 2 * CH] = jnp.ones((TOK, CH), BF16)

    def score(n):
        query = qs[n]
        for pair in range(2):
            masked = [
                jnp.where(head_of == pair * 2 + h, query, jnp.zeros_like(query)) for h in range(2)
            ]
            sbuf[n, pair * 512 : pair * 512 + 512, :] = dot(jnp.concatenate(masked, axis=0), ks[n], NT)

    @pl.loop(0, OWN)
    def _(il):
        project(il, il)

    score(0)
    along_line(0)
    score(1)
    along_line(1)
    along_line(2)

    @pl.loop(2, OWN)
    def _(n):
        score(n)

    swap.wait_recv()

    @pl.loop(0, OWN)
    def _(il):
        normed = layer_norm(upd[(1 - core) * OWN + il].reshape(TOK, CH).astype(F32)).astype(BF16)
        an[il] = normed.reshape(16, 2, 16, CH)
        project(OWN + il, il)

    @pl.loop(OWN, 2 * OWN)
    def _(n):
        score(n)

    for n, (ref, _, _, _) in enumerate(parts):
        settle(ref.at[0:3], l_recv.at[n])
    key_lane = lax.broadcasted_iota(jnp.int32, (1, TOK), 1)
    key_term = jnp.where(key_lane < count, 0.0, -1e9 * LOG2E)
    rows_u = 256 - 192 * core
    rows_v = 64 + 192 * core

    @pl.loop(0, LINE)
    def _(uu):
        for vv in range(LINE):
            for xx in range(LINE):
                rows = pl.ds(pl.multiple_of(uu * rows_u + vv * rows_v + xx * 16, 16), 16)
                pair = ba[uu, vv * LINE + xx]
                tiles = [pair[0:16], pair[16:32], bb[vv, uu * LINE + xx], bc[xx, uu * LINE + vv]]
                for kb, tile in enumerate(tiles):
                    cols = slice(kb * 128, kb * 128 + 128)
                    raw[kb, rows, :] = tile.astype(F32) * LOG2E + key_term[:, cols]

    for kb in range(LINE):
        for h in range(HEADS):
            bias[h, :, kb * 128 : kb * 128 + 128] = raw[kb, pl.ds(h, 256, stride=4), :]

    def attend(n, owner):
        weights = []
        for h in range(HEADS):
            for part in range(4):
                rows = slice(h * 256 + part * 64, h * 256 + part * 64 + 64)
                logits = sbuf[n, rows, :] + bias[h, part * 64 : part * 64 + 64, :]
                powers = jnp.exp2(logits - jnp.max(logits, axis=-1, keepdims=True))
                weights.append(powers.astype(BF16))
        mixed = dot(jnp.concatenate(weights, axis=0), vs[n])
        total = mixed[0:256]
        for h in range(1, HEADS):
            mask = jnp.concatenate([head_of, head_of], axis=1) == h
            total = jnp.where(mask, mixed[h * 256 : h * 256 + 256], total)
        attended = total[:, 0:CH] / total[:, CH : 2 * CH]
        gated = (attended * gs[n]).astype(BF16)
        before = upd[owner * OWN + n % OWN, :, core].reshape(256, CH).astype(F32)
        result = before + dot(gated, ao[...])
        osend[n] = result.astype(BF16).reshape(LINE, 4, 16, CH)
        target = out.at[q * OWN + n % OWN, :, core]
        for d in (2, 1, 3):
            remote(osend.at[n, xs[d]], target, o_send, o_recv, place(z, y, owner), xs[d]).start()

    @pl.loop(OWN, 2 * OWN)
    def _(n):
        attend(n, 1 - core)

    target = out.at[pl.ds(q * OWN, OWN), :, core]
    remote(osend.at[OWN : 2 * OWN, q], target, o_send, o_recv, twin, q).start()

    @pl.loop(0, OWN)
    def _(n):
        attend(n, core)

    pltpu.make_async_copy(osend.at[0:OWN, q], target, o_recv).start()

    settle(out, o_recv)
    settle(osend.at[0:7], o_send)

    @pl.when(core == 0)
    def _():
        settle(esend.at[0:3], e_send.at[0])
        settle(esend.at[0, 0 : 31 * 32], e_send.at[0])
        settle(tsend.at[0, 0 : 63 * 16], t_send.at[0])
        settle(tsend.at[1], t_send.at[1])

    @pl.when(core == 1)
    def _():
        settle(tsend.at[0], e_send.at[2])
        settle(tsend.at[0, 0 : 63 * 16], e_send.at[2])
        settle(tsend.at[0], t_send.at[0])
        settle(tsend.at[1, 0 : 63 * 16], t_send.at[1])

    swap.wait_send()
    for n, (ref, _, _, _) in enumerate(parts):
        settle(ref.at[0, 0:15], p_send.at[n])
        settle(ref.at[0:3], l_send.at[n])


def local(pair_act, valid_count, edge_proj, edge_gate, tri_gate, tri_out, attn_proj, bias_proj, attn_out):
    hbm = pl.BlockSpec(memory_space=pltpu.HBM)
    dma = pltpu.SemaphoreType.DMA
    return pl.pallas_call(
        kernel,
        out_shape=jax.ShapeDtypeStruct((ROWS, 4, 2, 16, CH), BF16),
        in_specs=[pl.BlockSpec(memory_space=pltpu.SMEM)] + [hbm] * 8,
        out_specs=pl.BlockSpec(memory_space=pl.ANY),
        scratch_shapes=[
            pltpu.VMEM((ROWS, COLS, CH), BF16),
            pltpu.VMEM((CH, 2 * CH), BF16),
            pltpu.VMEM((CH, 2 * CH), BF16),
            pltpu.VMEM((CH, CH), BF16),
            pltpu.VMEM((CH, CH), BF16),
            pltpu.VMEM((CH, 4 * CH), BF16),
            pltpu.VMEM((HEADS, CH), BF16),
            pltpu.VMEM((CH, CH), BF16),
            pltpu.VMEM((4, 128, CH), BF16),
            pltpu.VMEM((2048, CH), BF16),
            pltpu.VMEM((32 * 36, COLS), F32),
            pltpu.VMEM((4, 1024, COLS), BF16),
            pltpu.VMEM((LINE, 16, 2, 32, COLS), BF16),
            pltpu.VMEM((2, 1024, 128), F32),
            pltpu.VMEM((2, 1024, 128), BF16),
            pltpu.VMEM((CH, 16, 128), BF16),
            pltpu.VMEM((CH * 20, 128), F32),
            pltpu.VMEM((OWN, TOK, CH), F32),
            pltpu.VMEM((LINE, OWN, COLS, CH), BF16),
            pltpu.VMEM((2 * OWN, 16, 2, 16, CH), BF16),
            pltpu.VMEM((OWN, 16, 2, 16, CH), BF16),
            pltpu.VMEM((2 * OWN, 256, CH), BF16),
            pltpu.VMEM((2 * OWN, TOK, CH), BF16),
            pltpu.VMEM((2 * OWN, TOK, 2 * CH), BF16),
            pltpu.VMEM((2 * OWN, 256, CH), F32),
            pltpu.VMEM((LINE, 16, 32, 128), BF16),
            pltpu.VMEM((LINE, 16, 16, 128), BF16),
            pltpu.VMEM((LINE, 16, 16, 128), BF16),
            pltpu.VMEM((2 * OWN, 1024, TOK), F32),
            pltpu.VMEM((LINE, 1024, 128), F32),
            pltpu.VMEM((HEADS, 256, TOK), F32),
            pltpu.VMEM((2 * OWN, LINE, 4, 16, CH), BF16),
            pltpu.SemaphoreType.REGULAR, dma((8,)), dma((3,)), dma((3,)), dma, dma((3,)), dma((3,)), dma((2,)), dma,
            dma((3,)), dma((3,)), dma((3,)), dma((3,)), dma, dma, dma, dma,
        ],
        compiler_params=pltpu.CompilerParams(
            collective_id=0, has_side_effects=True, vmem_limit_bytes=63 * 1024 * 1024
        ),
        name="triangle",
    )(valid_count, pair_act, edge_proj, edge_gate, tri_gate, tri_out, attn_proj, bias_proj.T, attn_out).reshape(ROWS, COLS, CH)


def solution(mesh):
    placed = (P("row", "ch", None), P(), P(), P(), P(), P(), P(), P(), P())
    return jax.shard_map(
        local, mesh=mesh, in_specs=placed, out_specs=P("row", "ch", None), check_vma=False
    )
```

```python
import math

import jax
import jax.numpy as jnp
from jax import lax
from jax.experimental import pallas as pl
from jax.experimental.pallas import tpu as pltpu
from jax.sharding import PartitionSpec as P

MESH = pl.DeviceIdType.MESH
EPS = 1e-05
F32 = jnp.float32
BF16 = jnp.bfloat16
LOG2E = math.log2(math.e)
NT = (((1,), (1,)), ((), ()))
NN = (((1,), (0,)), ((), ()))

LINE = 4
ROWS = 16
COLS = 128
CH = 128
TOK = 512
HEADS = 4
HEAD = 32
OWN = 4
DEVICES = 128


OFFSETS = [
    (dz, dy, dc, dx) for dz in range(LINE) for dy in range(LINE) for dc in range(2) for dx in range(LINE)
][1:]


def hops(offset):
    dz, dy, _, dx = offset
    return sum(min(d, LINE - d) for d in (dz, dy, dx))


FAR_FIRST = sorted(OFFSETS, key=hops, reverse=True)


def dot(a, b, dims=NN):
    return lax.dot_general(a, b, dims, preferred_element_type=F32)


def sigmoid(x):
    return 0.5 * jnp.tanh(0.5 * x) + 0.5


def layer_norm(x):
    centre = x - jnp.mean(x, axis=-1, keepdims=True)
    spread = jnp.mean(centre * centre, axis=-1, keepdims=True)
    return centre * lax.rsqrt(spread + EPS)


def kernel(
    count_in, pa_in, ep_in, eg_in, tg_in, to_in, ap_in, bp_in, ao_in,
    out,
    count, pa, ep, eg, tg, to, ap, bp, ao, wt, nrm, ebuf, esend, lr, tst, tsend, trecv, tn, gbuf, a2, upd, an, qs, ks, vs, gs, ba, bb, bc, sbuf, raw, bias, osend,
    ready, load, pa_send, pa_recv, pa_own, e_send, e_recv, t_send, t_recv,
    p_send, p_recv, l_send, l_recv, u_send, u_recv, o_send, o_recv,
):
    r = lax.axis_index("row")
    q = lax.axis_index("ch")
    me = r * LINE + q
    z = lax.div(r, 8)
    y = lax.rem(lax.div(r, 2), 4)
    core = lax.rem(r, 2)

    def place(zz, yy, cc):
        return zz * 8 + yy * 2 + cc

    zs = [lax.rem(z + d, LINE) for d in range(LINE)]
    ys = [lax.rem(y + d, LINE) for d in range(LINE)]
    xs = [lax.rem(q + d, LINE) for d in range(LINE)]
    cores = [core, 1 - core]

    def peer(offset):
        dz, dy, dc, dx = offset
        return place(zs[dz], ys[dy], cores[dc]), xs[dx]

    def remote(src, dst, send, recv, rr, qq):
        return pltpu.make_async_remote_copy(
            src_ref=src, dst_ref=dst, send_sem=send, recv_sem=recv,
            device_id=(rr, qq), device_id_type=MESH,
        )

    def settle(ref, sem):
        pltpu.make_async_copy(ref, ref, sem).wait()

    loads = [
        pltpu.make_async_copy(src, dst, load.at[n])
        for n, (src, dst) in enumerate(
            [(count_in, count), (ep_in, ep), (eg_in, eg), (pa_in, pa), (tg_in, tg), (to_in, to), (ap_in, ap), (bp_in, bp), (ao_in, ao)]
        )
    ]
    for copy in loads:
        copy.start()

    barrier = pltpu.get_barrier_semaphore()

    plane = [o for o in OFFSETS if o[2] == 0 and o[3] == 0]
    near = [o for o in OFFSETS if o[0] == 0 and o[1] == 0] + plane
    for offset in near:
        rr, qq = peer(offset)
        pl.semaphore_signal(barrier, inc=1, device_id=(rr, qq), device_id_type=MESH)

    for copy in loads:
        copy.wait()

    @pl.loop(0, 4)
    def _(part):
        x = pa[pl.ds(part * 4, 4)].reshape(512, CH).astype(F32)
        nrm[pl.ds(pl.multiple_of(part * 512, 512), 512), :] = layer_norm(x).astype(BF16)

    pl.semaphore_wait(barrier, len(near))
    for offset in plane:
        rr, qq = peer(offset)
        pl.semaphore_signal(ready, inc=1, device_id=(rr, qq), device_id_type=MESH)

    spot = lax.broadcasted_iota(jnp.int32, (CH, CH), 0)
    line = spot % 32
    chosen = line * 4 + (spot // 32 + 8 - line // 8 - (line // 2) % 4) % 4
    order = (chosen == lax.broadcasted_iota(jnp.int32, (CH, CH), 1)).astype(BF16)
    for n, ref in enumerate((ep, ep, eg, eg)):
        side = n % 2
        part = dot(order, ref[:, side * CH : side * CH + CH], NT).astype(BF16)
        for m in range(4):
            wt[m, n * 32 : n * 32 + 32, :] = part[m * 32 : m * 32 + 32]
    lane = lax.broadcasted_iota(jnp.int32, (1, 512), 1)

    def edges_of(k):
        weights = wt[lax.rem(z + y + q + k, 4)]
        for part in range(4):
            both = dot(weights, nrm[part * 512 : part * 512 + 512, :], NT)
            row_token = r * ROWS + part * 4 + lane // 128
            col_token = q * COLS + lane % 128
            valid = jnp.where((row_token < count[...]) & (col_token < count[...]), 1.0, 0.0)
            edges = sigmoid(both[64:128]) * both[0:64] * valid
            for i in range(4):
                for side in range(2):
                    ebuf[pl.ds(side * 16 + part * 4 + i, 32, stride=36), :] = edges[
                        side * 32 : side * 32 + 32, i * 128 : i * 128 + 128
                    ]
        for n in range(32):
            esend[k, n * 32 : n * 32 + 32, :] = ebuf[n * 36 : n * 36 + 32, :].astype(BF16)

    for step, k in enumerate((2, 1, 3, 0)):
        edges_of(k)
        if step == 0:
            pl.semaphore_wait(ready, len(plane))
        targets = [o for o in FAR_FIRST if (o[0] + o[1] + o[3]) % 4 == k]

        @pl.when(core == 0)
        def _():
            for offset in targets:
                rr, qq = peer(offset)
                rows = pl.ds(pl.multiple_of(rr * 32, 32), 32)
                remote(esend.at[k, rows], lr.at[q, z * LINE + y, 0], e_send.at[0], e_recv.at[0], rr, qq).start()

        @pl.when(core == 1)
        def _():
            for offset in targets:
                rr, qq = peer(offset)
                rows = pl.ds(pl.multiple_of(rr * 32 + 16, 16), 16)
                remote(
                    esend.at[k, rows], lr.at[q, z * LINE + y, 1, 16:32], e_send.at[1], e_recv.at[1], rr, qq
                ).start()

    @pl.when(core == 0)
    def _():
        own = pl.ds(pl.multiple_of(r * 32, 32), 32)
        pltpu.make_async_copy(esend.at[0, own], lr.at[q, z * LINE + y, 0], e_recv.at[0]).start()

    @pl.when(core == 1)
    def _():
        own = pl.ds(pl.multiple_of(r * 32 + 16, 16), 16)
        pltpu.make_async_copy(esend.at[0, own], lr.at[q, z * LINE + y, 1, 16:32], e_recv.at[1]).start()
        settle(tsend.at[0], e_send.at[1])
        settle(tsend.at[0, 0 : 63 * 16], e_send.at[1])
        for offset in FAR_FIRST:
            rr, qq = peer(offset)
            rows = pl.ds(pl.multiple_of(rr * 32, 32), 16)
            k = (offset[0] + offset[1] + offset[3]) % 4
            remote(
                esend.at[k, rows], lr.at[q, z * LINE + y, 1, 0:16], e_send.at[2], e_recv.at[2], rr, qq
            ).start()
        own = pl.ds(pl.multiple_of(r * 32, 32), 16)
        pltpu.make_async_copy(esend.at[0, own], lr.at[q, z * LINE + y, 1, 0:16], e_recv.at[2]).start()

    pa_copies = []
    for dq in range(1, LINE):
        qq = lax.rem(q + dq, LINE)
        copy = remote(
            pa.at[pl.ds(qq * OWN, OWN)], a2.at[q], pa_send.at[dq - 1], pa_recv.at[dq - 1], r, qq
        )
        copy.start()
        pa_copies.append(copy)
    pa_local = pltpu.make_async_copy(pa.at[pl.ds(q * OWN, OWN)], a2.at[q], pa_own)
    pa_local.start()

    settle(lr.at[:, :, 0], e_recv.at[0])
    settle(lr.at[:, :, 1, 16:32], e_recv.at[1])
    right = jnp.concatenate([lr[k, :, :, 16:32, :].reshape(TOK, COLS) for k in range(LINE)], axis=1)
    for half in range(2):
        if half == 1:
            settle(lr.at[:, :, 1, 0:16], e_recv.at[2])
        left = jnp.concatenate(
            [lr[k, :, half, 0:16, :].reshape(256, COLS) for k in range(LINE)], axis=1
        )
        tri = dot(left, right, NT)
        for jb in range(LINE):
            tst[half, pl.ds(jb, 256, stride=4), :] = tri[:, jb * 128 : jb * 128 + 128]
        tsend[half] = tst[half].astype(BF16)
        for offset in FAR_FIRST:
            if offset[2] == 0:
                zz, yy, qq = zs[offset[0]], ys[offset[1]], xs[offset[3]]
                rows = pl.ds(pl.multiple_of((zz * 16 + yy * 4 + qq) * 16, 16), 16)
                remote(
                    tsend.at[half, rows], trecv.at[me], t_send.at[half], t_recv, place(zz, yy, half), qq
                ).start()
        own = pl.ds(pl.multiple_of((z * 16 + y * 4 + q) * 16, 16), 16)

        @pl.when(core == half)
        def _():
            pltpu.make_async_copy(tsend.at[half, own], trecv.at[me], t_recv).start()

        @pl.when(core != half)
        def _():
            remote(
                tsend.at[half, own], trecv.at[me], t_send.at[half], t_recv, place(z, y, half), q
            ).start()

    pa_local.wait()
    for copy in pa_copies:
        copy.wait()

    @pl.loop(0, OWN)
    def _(jb):
        x = a2[jb].reshape(TOK, CH).astype(F32)
        gbuf[jb] = sigmoid(dot(layer_norm(x).astype(BF16), tg[...]))

    settle(trecv, t_recv)

    def add(part, total):
        return total + jnp.sum(trecv[pl.ds(part * 16, 16)].astype(F32), axis=0)

    mean = lax.fori_loop(0, 8, add, jnp.zeros((16, 128), F32)) * (1.0 / CH)

    def add_square(part, total):
        centre = trecv[pl.ds(part * 16, 16)].astype(F32) - mean[None]
        return total + jnp.sum(centre * centre, axis=0)

    spread = lax.fori_loop(0, 8, add_square, jnp.zeros((16, 128), F32)) * (1.0 / CH)
    gain = lax.rsqrt(spread + EPS)

    @pl.loop(0, 8)
    def _(part):
        block = (trecv[pl.ds(part * 16, 16)].astype(F32) - mean[None]) * gain[None]
        for n in range(16):
            tn[pl.ds(part * 320 + n * 20, 16), :] = block[n]

    spot = lax.broadcasted_iota(jnp.int32, (16, HEADS), 0) % HEADS
    pick = (spot == lax.broadcasted_iota(jnp.int32, (16, HEADS), 1)).astype(BF16)
    bias_w = dot(pick, bp[...]).astype(BF16)
    bias_row = lax.broadcasted_iota(jnp.int32, (16, 128), 0) // HEADS

    u = z + core * (y - z)
    v = y + core * (z - y)
    us = [lax.rem(u + d, LINE) for d in range(LINE)]
    vvs = [lax.rem(v + d, LINE) for d in range(LINE)]
    step_u = 8 - 6 * core
    step_v = 2 + 6 * core
    parts = [(ba, us, vvs, xs), (bb, vvs, us, xs), (bc, xs, us, vvs)]

    def at(n, line, first, second):
        uu, vv, xx = [
            (us[line], vvs[first], xs[second]),
            (us[first], vvs[line], xs[second]),
            (us[first], vvs[second], xs[line]),
        ][n]
        return uu * step_u + vv * step_v + core, xx

    def over_plane(n):
        ref, lines, firsts, seconds = parts[n]
        slot = ref.at[lines[0], firsts[0] * LINE + seconds[0]]
        pairs = [(f, t) for f in range(LINE) for t in range(LINE)][1:]
        for f, t in sorted(pairs, key=lambda p: -min(p[0], LINE - p[0]) - min(p[1], LINE - p[1])):
            remote(slot, slot, p_send.at[n], p_recv.at[n * LINE + f], *at(n, 0, f, t)).start()

    def along_line(n, f):
        ref, lines, firsts, _ = parts[n]
        settle(ref.at[lines[0], 0 : 3 if f == 0 else 4], p_recv.at[n * LINE + f])
        entries = pl.ds(firsts[(LINE - f) % LINE] * LINE, LINE)
        for d in (2, 1, 3):
            slot = ref.at[lines[0], entries]
            remote(slot, slot, l_send.at[n], l_recv.at[n], *at(n, d, 0, 0)).start()

    mine = pl.ds(core * OWN, OWN)
    for jb in range(LINE):
        blocks = [
            tn[pl.ds(il * LINE + jb, 128, stride=20), :].T.astype(BF16) for il in range(OWN)
        ]
        product = dot(jnp.concatenate(blocks, axis=0), to[...])
        x = a2[jb].reshape(TOK, CH).astype(F32)
        updated = (x + gbuf[jb] * product).astype(BF16)
        upd[mine, jb * 4 : jb * 4 + 4] = updated.reshape(OWN, 4, 2, 16, CH)
        normed = layer_norm(updated.astype(F32)).astype(BF16)
        an[:, jb * 4 : jb * 4 + 4] = normed.reshape(OWN, 4, 2, 16, CH)
        biases = dot(bias_w, normed, NT)
        tile = biases[:, 0:128]
        for il in range(1, OWN):
            tile = jnp.where(bias_row == il, biases[:, il * 128 : il * 128 + 128], tile)
        tile = tile.astype(BF16)
        if jb < 2:
            ba[u, v * LINE + q, jb * 16 : jb * 16 + 16, :] = tile
        elif jb == 2:
            bb[v, u * LINE + q] = tile
        else:
            bc[q, u * LINE + v] = tile
        if jb == 1:
            over_plane(0)
    over_plane(1)
    over_plane(2)

    twin = place(z, y, 1 - core)
    swap = remote(upd.at[mine], upd.at[mine], u_send, u_recv, twin, q)
    swap.start()

    head_of = lax.broadcasted_iota(jnp.int32, (256, CH), 1) // HEAD

    def project(n, il):
        half = an[il, :, core].reshape(256, CH)
        qs[n] = (dot(half, ap[:, 0:CH]) * (HEAD**-0.5 * LOG2E)).astype(BF16)
        gs[n] = sigmoid(dot(half, ap[:, 3 * CH : 4 * CH]))
        mixed = dot(an[il].reshape(TOK, CH), ap[:, CH : 3 * CH])
        ks[n] = mixed[:, 0:CH].astype(BF16)
        vs[n, :, 0:CH] = mixed[:, CH : 2 * CH].astype(BF16)
        vs[n, :, CH : 2 * CH] = jnp.ones((TOK, CH), BF16)

    def score(n):
        query = qs[n]
        for pair in range(2):
            masked = [
                jnp.where(head_of == pair * 2 + h, query, jnp.zeros_like(query)) for h in range(2)
            ]
            sbuf[n, pair * 512 : pair * 512 + 512, :] = dot(jnp.concatenate(masked, axis=0), ks[n], NT)

    @pl.loop(0, OWN)
    def _(il):
        project(il, il)

    for f in (0, 1):
        for n in range(3):
            along_line(n, f)
    score(0)
    for n in range(3):
        along_line(n, 3)
    score(1)
    for n in range(3):
        along_line(n, 2)

    @pl.loop(2, OWN)
    def _(n):
        score(n)

    swap.wait_recv()

    @pl.loop(0, OWN)
    def _(il):
        normed = layer_norm(upd[(1 - core) * OWN + il].reshape(TOK, CH).astype(F32)).astype(BF16)
        an[il] = normed.reshape(16, 2, 16, CH)
        project(OWN + il, il)

    @pl.loop(OWN, 2 * OWN)
    def _(n):
        score(n)

    for n, (ref, _, _, _) in enumerate(parts):
        settle(ref.at[0:3], l_recv.at[n])
    key_lane = lax.broadcasted_iota(jnp.int32, (1, TOK), 1)
    key_term = jnp.where(key_lane < count[...], 0.0, -1e9 * LOG2E)
    rows_u = 256 - 192 * core
    rows_v = 64 + 192 * core

    @pl.loop(0, LINE)
    def _(uu):
        for vv in range(LINE):
            for xx in range(LINE):
                rows = pl.ds(pl.multiple_of(uu * rows_u + vv * rows_v + xx * 16, 16), 16)
                pair = ba[uu, vv * LINE + xx]
                tiles = [pair[0:16], pair[16:32], bb[vv, uu * LINE + xx], bc[xx, uu * LINE + vv]]
                for kb, tile in enumerate(tiles):
                    cols = slice(kb * 128, kb * 128 + 128)
                    raw[kb, rows, :] = tile.astype(F32) * LOG2E + key_term[:, cols]

    for kb in range(LINE):
        for h in range(HEADS):
            bias[h, :, kb * 128 : kb * 128 + 128] = raw[kb, pl.ds(h, 256, stride=4), :]

    def attend(n, owner):
        weights = []
        for h in range(HEADS):
            for part in range(4):
                rows = slice(h * 256 + part * 64, h * 256 + part * 64 + 64)
                logits = sbuf[n, rows, :] + bias[h, part * 64 : part * 64 + 64, :]
                powers = jnp.exp2(logits - jnp.max(logits, axis=-1, keepdims=True))
                weights.append(powers.astype(BF16))
        mixed = dot(jnp.concatenate(weights, axis=0), vs[n])
        total = mixed[0:256]
        for h in range(1, HEADS):
            mask = jnp.concatenate([head_of, head_of], axis=1) == h
            total = jnp.where(mask, mixed[h * 256 : h * 256 + 256], total)
        attended = total[:, 0:CH] / total[:, CH : 2 * CH]
        gated = (attended * gs[n]).astype(BF16)
        before = upd[owner * OWN + n % OWN, :, core].reshape(256, CH).astype(F32)
        result = before + dot(gated, ao[...])
        osend[n] = result.astype(BF16).reshape(LINE, 4, 16, CH)
        target = out.at[q * OWN + n % OWN, :, core]
        for d in (2, 1, 3):
            remote(osend.at[n, xs[d]], target, o_send, o_recv, place(z, y, owner), xs[d]).start()

    @pl.loop(OWN, 2 * OWN)
    def _(n):
        attend(n, 1 - core)

    target = out.at[pl.ds(q * OWN, OWN), :, core]
    remote(osend.at[OWN : 2 * OWN, q], target, o_send, o_recv, twin, q).start()

    @pl.loop(0, OWN)
    def _(n):
        attend(n, core)

    pltpu.make_async_copy(osend.at[0:OWN, q], target, o_recv).start()

    settle(out, o_recv)
    settle(osend.at[0:7], o_send)

    @pl.when(core == 0)
    def _():
        settle(esend.at[0:3], e_send.at[0])
        settle(esend.at[0, 0 : 31 * 32], e_send.at[0])
        settle(tsend.at[0, 0 : 63 * 16], t_send.at[0])
        settle(tsend.at[1], t_send.at[1])

    @pl.when(core == 1)
    def _():
        settle(tsend.at[0], e_send.at[2])
        settle(tsend.at[0, 0 : 63 * 16], e_send.at[2])
        settle(tsend.at[0], t_send.at[0])
        settle(tsend.at[1, 0 : 63 * 16], t_send.at[1])

    swap.wait_send()
    for n, (ref, _, _, _) in enumerate(parts):
        settle(ref.at[0, 0:15], p_send.at[n])
        settle(ref.at[0:3], l_send.at[n])


def local(pair_act, valid_count, edge_proj, edge_gate, tri_gate, tri_out, attn_proj, bias_proj, attn_out):
    hbm = pl.BlockSpec(memory_space=pltpu.HBM)
    dma = pltpu.SemaphoreType.DMA
    return pl.pallas_call(
        kernel,
        out_shape=jax.ShapeDtypeStruct((ROWS, 4, 2, 16, CH), BF16),
        in_specs=[hbm] * 9,
        out_specs=pl.BlockSpec(memory_space=pl.ANY),
        scratch_shapes=[
            pltpu.VMEM((1, 1), jnp.int32),
            pltpu.VMEM((ROWS, COLS, CH), BF16),
            pltpu.VMEM((CH, 2 * CH), BF16),
            pltpu.VMEM((CH, 2 * CH), BF16),
            pltpu.VMEM((CH, CH), BF16),
            pltpu.VMEM((CH, CH), BF16),
            pltpu.VMEM((CH, 4 * CH), BF16),
            pltpu.VMEM((HEADS, CH), BF16),
            pltpu.VMEM((CH, CH), BF16),
            pltpu.VMEM((4, 128, CH), BF16),
            pltpu.VMEM((2048, CH), BF16),
            pltpu.VMEM((32 * 36, COLS), F32),
            pltpu.VMEM((4, 1024, COLS), BF16),
            pltpu.VMEM((LINE, 16, 2, 32, COLS), BF16),
            pltpu.VMEM((2, 1024, 128), F32),
            pltpu.VMEM((2, 1024, 128), BF16),
            pltpu.VMEM((CH, 16, 128), BF16),
            pltpu.VMEM((CH * 20, 128), F32),
            pltpu.VMEM((OWN, TOK, CH), F32),
            pltpu.VMEM((LINE, OWN, COLS, CH), BF16),
            pltpu.VMEM((2 * OWN, 16, 2, 16, CH), BF16),
            pltpu.VMEM((OWN, 16, 2, 16, CH), BF16),
            pltpu.VMEM((2 * OWN, 256, CH), BF16),
            pltpu.VMEM((2 * OWN, TOK, CH), BF16),
            pltpu.VMEM((2 * OWN, TOK, 2 * CH), BF16),
            pltpu.VMEM((2 * OWN, 256, CH), F32),
            pltpu.VMEM((LINE, 16, 32, 128), BF16),
            pltpu.VMEM((LINE, 16, 16, 128), BF16),
            pltpu.VMEM((LINE, 16, 16, 128), BF16),
            pltpu.VMEM((2 * OWN, 1024, TOK), F32),
            pltpu.VMEM((LINE, 1024, 128), F32),
            pltpu.VMEM((HEADS, 256, TOK), F32),
            pltpu.VMEM((2 * OWN, LINE, 4, 16, CH), BF16),
            pltpu.SemaphoreType.REGULAR, dma((9,)), dma((3,)), dma((3,)), dma, dma((3,)), dma((3,)), dma((2,)), dma,
            dma((3,)), dma((12,)), dma((3,)), dma((3,)), dma, dma, dma, dma,
        ],
        compiler_params=pltpu.CompilerParams(
            collective_id=0, has_side_effects=True, vmem_limit_bytes=48 * 1024 * 1024
        ),
        name="triangle",
    )(valid_count.reshape(1, 1), *[pltpu.with_memory_space_constraint(a, pltpu.HBM) for a in (pair_act, edge_proj, edge_gate, tri_gate, tri_out, attn_proj, bias_proj.T, attn_out)]).reshape(ROWS, COLS, CH)


def solution(mesh):
    placed = (P("row", "ch", None), P(), P(), P(), P(), P(), P(), P(), P())
    return jax.shard_map(
        local, mesh=mesh, in_specs=placed, out_specs=P("row", "ch", None), check_vma=False
    )
```

```python
import math

import jax
import jax.numpy as jnp
from jax import lax
from jax.experimental import pallas as pl
from jax.experimental.pallas import tpu as pltpu
from jax.sharding import PartitionSpec as P

MESH = pl.DeviceIdType.MESH
EPS = 1e-05
F32 = jnp.float32
BF16 = jnp.bfloat16
LOG2E = math.log2(math.e)
NT = (((1,), (1,)), ((), ()))
NN = (((1,), (0,)), ((), ()))

LINE = 4
ROWS = 16
COLS = 128
CH = 128
TOK = 512
HEADS = 4
HEAD = 32
OWN = 4
DEVICES = 128


OFFSETS = [
    (dz, dy, dc, dx) for dz in range(LINE) for dy in range(LINE) for dc in range(2) for dx in range(LINE)
][1:]


def hops(offset):
    dz, dy, _, dx = offset
    return sum(min(d, LINE - d) for d in (dz, dy, dx))


FAR_FIRST = sorted(OFFSETS, key=hops, reverse=True)


def dot(a, b, dims=NN):
    return lax.dot_general(a, b, dims, preferred_element_type=F32)


def sigmoid(x):
    return 0.5 * jnp.tanh(0.5 * x) + 0.5


def layer_norm(x):
    centre = x - jnp.mean(x, axis=-1, keepdims=True)
    spread = jnp.mean(centre * centre, axis=-1, keepdims=True)
    return centre * lax.rsqrt(spread + EPS)


def kernel(
    count_in, pa_in, ep_in, eg_in, tg_in, to_in, ap_in, bp_in, ao_in,
    out,
    count, pa, ep, eg, tg, to, ap, bp, ao, wt, nrm, ebuf, esend, lr, tst, tsend, trecv, tn, gbuf, a2, upd, an, qs, ks, vs, gs, ba, bb, bc, sbuf, raw, bias, osend,
    ready, load, pa_send, pa_recv, pa_own, e_send, e_recv, t_send, t_recv,
    p_send, p_recv, l_send, l_recv, u_send, u_recv, o_send, o_recv,
):
    r = lax.axis_index("row")
    q = lax.axis_index("ch")
    me = r * LINE + q
    z = lax.div(r, 8)
    y = lax.rem(lax.div(r, 2), 4)
    core = lax.rem(r, 2)

    def place(zz, yy, cc):
        return zz * 8 + yy * 2 + cc

    zs = [lax.rem(z + d, LINE) for d in range(LINE)]
    ys = [lax.rem(y + d, LINE) for d in range(LINE)]
    xs = [lax.rem(q + d, LINE) for d in range(LINE)]
    cores = [core, 1 - core]

    def peer(offset):
        dz, dy, dc, dx = offset
        return place(zs[dz], ys[dy], cores[dc]), xs[dx]

    def remote(src, dst, send, recv, rr, qq):
        return pltpu.make_async_remote_copy(
            src_ref=src, dst_ref=dst, send_sem=send, recv_sem=recv,
            device_id=(rr, qq), device_id_type=MESH,
        )

    def settle(ref, sem):
        pltpu.make_async_copy(ref, ref, sem).wait()

    barrier = pltpu.get_barrier_semaphore()

    plane = [o for o in OFFSETS if o[2] == 0 and o[3] == 0]
    near = [o for o in OFFSETS if o[0] == 0 and o[1] == 0] + plane
    for offset in near:
        rr, qq = peer(offset)
        pl.semaphore_signal(barrier, inc=1, device_id=(rr, qq), device_id_type=MESH)

    loads = [
        pltpu.make_async_copy(src, dst, load.at[n])
        for n, (src, dst) in enumerate(
            [(count_in, count), (ep_in, ep), (eg_in, eg), (pa_in, pa), (tg_in, tg), (to_in, to), (ap_in, ap), (bp_in, bp), (ao_in, ao)]
        )
    ]
    for copy in loads:
        copy.start()

    for copy in loads:
        copy.wait()

    @pl.loop(0, 4)
    def _(part):
        x = pa[pl.ds(part * 4, 4)].reshape(512, CH).astype(F32)
        nrm[pl.ds(pl.multiple_of(part * 512, 512), 512), :] = layer_norm(x).astype(BF16)

    pl.semaphore_wait(barrier, len(near))
    for offset in plane:
        rr, qq = peer(offset)
        pl.semaphore_signal(ready, inc=1, device_id=(rr, qq), device_id_type=MESH)

    spot = lax.broadcasted_iota(jnp.int32, (CH, CH), 0)
    line = spot % 32
    chosen = line * 4 + (spot // 32 + 8 - line // 8 - (line // 2) % 4) % 4
    order = (chosen == lax.broadcasted_iota(jnp.int32, (CH, CH), 1)).astype(BF16)
    for n, ref in enumerate((ep, ep, eg, eg)):
        side = n % 2
        part = dot(order, ref[:, side * CH : side * CH + CH], NT).astype(BF16)
        for m in range(4):
            wt[m, n * 32 : n * 32 + 32, :] = part[m * 32 : m * 32 + 32]
    lane = lax.broadcasted_iota(jnp.int32, (1, 512), 1)

    def edges_of(k):
        weights = wt[lax.rem(z + y + q + k, 4)]
        for part in range(4):
            both = dot(weights, nrm[part * 512 : part * 512 + 512, :], NT)
            row_token = r * ROWS + part * 4 + lane // 128
            col_token = q * COLS + lane % 128
            valid = jnp.where((row_token < count[...]) & (col_token < count[...]), 1.0, 0.0)
            edges = sigmoid(both[64:128]) * both[0:64] * valid
            for i in range(4):
                for side in range(2):
                    ebuf[pl.ds(side * 16 + part * 4 + i, 32, stride=36), :] = edges[
                        side * 32 : side * 32 + 32, i * 128 : i * 128 + 128
                    ]
        for n in range(32):
            esend[k, n * 32 : n * 32 + 32, :] = ebuf[n * 36 : n * 36 + 32, :].astype(BF16)

    for step, k in enumerate((2, 1, 3, 0)):
        edges_of(k)
        if step == 0:
            pl.semaphore_wait(ready, len(plane))
        targets = [o for o in FAR_FIRST if (o[0] + o[1] + o[3]) % 4 == k]

        @pl.when(core == 0)
        def _():
            for offset in targets:
                rr, qq = peer(offset)
                rows = pl.ds(pl.multiple_of(rr * 32, 32), 32)
                remote(esend.at[k, rows], lr.at[q, z * LINE + y, 0], e_send.at[0], e_recv.at[0], rr, qq).start()

        @pl.when(core == 1)
        def _():
            for offset in targets:
                rr, qq = peer(offset)
                rows = pl.ds(pl.multiple_of(rr * 32 + 16, 16), 16)
                remote(
                    esend.at[k, rows], lr.at[q, z * LINE + y, 1, 16:32], e_send.at[1], e_recv.at[1], rr, qq
                ).start()

    @pl.when(core == 0)
    def _():
        own = pl.ds(pl.multiple_of(r * 32, 32), 32)
        pltpu.make_async_copy(esend.at[0, own], lr.at[q, z * LINE + y, 0], e_recv.at[0]).start()

    @pl.when(core == 1)
    def _():
        own = pl.ds(pl.multiple_of(r * 32 + 16, 16), 16)
        pltpu.make_async_copy(esend.at[0, own], lr.at[q, z * LINE + y, 1, 16:32], e_recv.at[1]).start()
        settle(tsend.at[0], e_send.at[1])
        settle(tsend.at[0, 0 : 63 * 16], e_send.at[1])
        for offset in FAR_FIRST:
            rr, qq = peer(offset)
            rows = pl.ds(pl.multiple_of(rr * 32, 32), 16)
            k = (offset[0] + offset[1] + offset[3]) % 4
            remote(
                esend.at[k, rows], lr.at[q, z * LINE + y, 1, 0:16], e_send.at[2], e_recv.at[2], rr, qq
            ).start()
        own = pl.ds(pl.multiple_of(r * 32, 32), 16)
        pltpu.make_async_copy(esend.at[0, own], lr.at[q, z * LINE + y, 1, 0:16], e_recv.at[2]).start()

    pa_copies = []
    for dq in range(1, LINE):
        qq = lax.rem(q + dq, LINE)
        copy = remote(
            pa.at[pl.ds(qq * OWN, OWN)], a2.at[q], pa_send.at[dq - 1], pa_recv.at[dq - 1], r, qq
        )
        copy.start()
        pa_copies.append(copy)
    pa_local = pltpu.make_async_copy(pa.at[pl.ds(q * OWN, OWN)], a2.at[q], pa_own)
    pa_local.start()

    settle(lr.at[:, :, 0], e_recv.at[0])
    settle(lr.at[:, :, 1, 16:32], e_recv.at[1])
    right = jnp.concatenate([lr[k, :, :, 16:32, :].reshape(TOK, COLS) for k in range(LINE)], axis=1)
    for half in range(2):
        if half == 1:
            settle(lr.at[:, :, 1, 0:16], e_recv.at[2])
        left = jnp.concatenate(
            [lr[k, :, half, 0:16, :].reshape(256, COLS) for k in range(LINE)], axis=1
        )
        tri = dot(left, right, NT)
        for jb in range(LINE):
            tst[half, pl.ds(jb, 256, stride=4), :] = tri[:, jb * 128 : jb * 128 + 128]
        tsend[half] = tst[half].astype(BF16)
        for offset in FAR_FIRST:
            if offset[2] == 0:
                zz, yy, qq = zs[offset[0]], ys[offset[1]], xs[offset[3]]
                rows = pl.ds(pl.multiple_of((zz * 16 + yy * 4 + qq) * 16, 16), 16)
                remote(
                    tsend.at[half, rows], trecv.at[me], t_send.at[half], t_recv, place(zz, yy, half), qq
                ).start()
        own = pl.ds(pl.multiple_of((z * 16 + y * 4 + q) * 16, 16), 16)

        @pl.when(core == half)
        def _():
            pltpu.make_async_copy(tsend.at[half, own], trecv.at[me], t_recv).start()

        @pl.when(core != half)
        def _():
            remote(
                tsend.at[half, own], trecv.at[me], t_send.at[half], t_recv, place(z, y, half), q
            ).start()

    spot = lax.broadcasted_iota(jnp.int32, (16, HEADS), 0) % HEADS
    pick = (spot == lax.broadcasted_iota(jnp.int32, (16, HEADS), 1)).astype(BF16)
    bias_w = dot(pick, bp[...]).astype(BF16)
    bias_row = lax.broadcasted_iota(jnp.int32, (16, 128), 0) // HEADS

    pa_local.wait()
    for copy in pa_copies:
        copy.wait()

    @pl.loop(0, OWN)
    def _(jb):
        x = a2[jb].reshape(TOK, CH).astype(F32)
        gbuf[jb] = sigmoid(dot(layer_norm(x).astype(BF16), tg[...]))

    settle(trecv, t_recv)

    def add(part, total):
        return total + jnp.sum(trecv[pl.ds(part * 32, 32)].astype(F32), axis=0)

    mean = lax.fori_loop(0, 4, add, jnp.zeros((16, 128), F32)) * (1.0 / CH)

    def add_square(part, total):
        centre = trecv[pl.ds(part * 32, 32)].astype(F32) - mean[None]
        return total + jnp.sum(centre * centre, axis=0)

    spread = lax.fori_loop(0, 4, add_square, jnp.zeros((16, 128), F32)) * (1.0 / CH)
    gain = lax.rsqrt(spread + EPS)

    @pl.loop(0, 8)
    def _(part):
        block = (trecv[pl.ds(part * 16, 16)].astype(F32) - mean[None]) * gain[None]
        for n in range(16):
            tn[pl.ds(part * 320 + n * 20, 16), :] = block[n]

    u = z + core * (y - z)
    v = y + core * (z - y)
    us = [lax.rem(u + d, LINE) for d in range(LINE)]
    vvs = [lax.rem(v + d, LINE) for d in range(LINE)]
    step_u = 8 - 6 * core
    step_v = 2 + 6 * core
    parts = [(ba, us, vvs, xs), (bb, vvs, us, xs), (bc, xs, us, vvs)]

    def at(n, line, first, second):
        uu, vv, xx = [
            (us[line], vvs[first], xs[second]),
            (us[first], vvs[line], xs[second]),
            (us[first], vvs[second], xs[line]),
        ][n]
        return uu * step_u + vv * step_v + core, xx

    def over_plane(n):
        ref, lines, firsts, seconds = parts[n]
        slot = ref.at[lines[0], firsts[0] * LINE + seconds[0]]
        pairs = [(f, t) for f in range(LINE) for t in range(LINE)][1:]
        for f, t in sorted(pairs, key=lambda p: -min(p[0], LINE - p[0]) - min(p[1], LINE - p[1])):
            remote(slot, slot, p_send.at[n], p_recv.at[n * LINE + f], *at(n, 0, f, t)).start()

    def along_line(n, f):
        ref, lines, firsts, _ = parts[n]
        settle(ref.at[lines[0], 0 : 3 if f == 0 else 4], p_recv.at[n * LINE + f])
        entries = pl.ds(firsts[(LINE - f) % LINE] * LINE, LINE)
        for d in (2, 1, 3):
            slot = ref.at[lines[0], entries]
            remote(slot, slot, l_send.at[n], l_recv.at[n], *at(n, d, 0, 0)).start()

    mine = pl.ds(core * OWN, OWN)
    for jb in range(LINE):
        blocks = [
            tn[pl.ds(il * LINE + jb, 128, stride=20), :].T.astype(BF16) for il in range(OWN)
        ]
        product = dot(jnp.concatenate(blocks, axis=0), to[...])
        x = a2[jb].reshape(TOK, CH).astype(F32)
        updated = (x + gbuf[jb] * product).astype(BF16)
        upd[mine, jb * 4 : jb * 4 + 4] = updated.reshape(OWN, 4, 2, 16, CH)
        normed = layer_norm(updated.astype(F32)).astype(BF16)
        an[:, jb * 4 : jb * 4 + 4] = normed.reshape(OWN, 4, 2, 16, CH)
        biases = dot(bias_w, normed, NT)
        tile = biases[:, 0:128]
        for il in range(1, OWN):
            tile = jnp.where(bias_row == il, biases[:, il * 128 : il * 128 + 128], tile)
        tile = tile.astype(BF16)
        if jb < 2:
            ba[u, v * LINE + q, jb * 16 : jb * 16 + 16, :] = tile
        elif jb == 2:
            bb[v, u * LINE + q] = tile
        else:
            bc[q, u * LINE + v] = tile
        if jb == 1:
            over_plane(0)
    over_plane(1)
    over_plane(2)

    twin = place(z, y, 1 - core)
    swap = remote(upd.at[mine], upd.at[mine], u_send, u_recv, twin, q)
    swap.start()

    head_of = lax.broadcasted_iota(jnp.int32, (256, CH), 1) // HEAD

    def project(n, il):
        half = an[il, :, core].reshape(256, CH)
        qs[n] = (dot(half, ap[:, 0:CH]) * (HEAD**-0.5 * LOG2E)).astype(BF16)
        gs[n] = sigmoid(dot(half, ap[:, 3 * CH : 4 * CH]))
        mixed = dot(an[il].reshape(TOK, CH), ap[:, CH : 3 * CH])
        ks[n] = mixed[:, 0:CH].astype(BF16)
        vs[n, :, 0:CH] = mixed[:, CH : 2 * CH].astype(BF16)
        vs[n, :, CH : 2 * CH] = jnp.ones((TOK, CH), BF16)

    def score(n):
        query = qs[n]
        for pair in range(2):
            masked = [
                jnp.where(head_of == pair * 2 + h, query, jnp.zeros_like(query)) for h in range(2)
            ]
            sbuf[n, pair * 512 : pair * 512 + 512, :] = dot(jnp.concatenate(masked, axis=0), ks[n], NT)

    @pl.loop(0, OWN)
    def _(il):
        project(il, il)

    for f in (0, 1):
        for n in range(3):
            along_line(n, f)
    score(0)
    for n in range(3):
        along_line(n, 3)
    score(1)
    for n in range(3):
        along_line(n, 2)

    @pl.loop(2, OWN)
    def _(n):
        score(n)

    swap.wait_recv()

    @pl.loop(0, OWN)
    def _(il):
        normed = layer_norm(upd[(1 - core) * OWN + il].reshape(TOK, CH).astype(F32)).astype(BF16)
        an[il] = normed.reshape(16, 2, 16, CH)
        project(OWN + il, il)

    @pl.loop(OWN, 2 * OWN)
    def _(n):
        score(n)

    for n, (ref, _, _, _) in enumerate(parts):
        settle(ref.at[0:3], l_recv.at[n])
    key_lane = lax.broadcasted_iota(jnp.int32, (1, TOK), 1)
    key_term = jnp.where(key_lane < count[...], 0.0, -1e9 * LOG2E)
    rows_u = 256 - 192 * core
    rows_v = 64 + 192 * core

    @pl.loop(0, LINE)
    def _(uu):
        for vv in range(LINE):
            for xx in range(LINE):
                rows = pl.ds(pl.multiple_of(uu * rows_u + vv * rows_v + xx * 16, 16), 16)
                pair = ba[uu, vv * LINE + xx]
                tiles = [pair[0:16], pair[16:32], bb[vv, uu * LINE + xx], bc[xx, uu * LINE + vv]]
                for kb, tile in enumerate(tiles):
                    cols = slice(kb * 128, kb * 128 + 128)
                    raw[kb, rows, :] = tile.astype(F32) * LOG2E + key_term[:, cols]

    for kb in range(LINE):
        for h in range(HEADS):
            bias[h, :, kb * 128 : kb * 128 + 128] = raw[kb, pl.ds(h, 256, stride=4), :]

    def attend(n, owner):
        weights = []
        for h in range(HEADS):
            for part in range(4):
                rows = slice(h * 256 + part * 64, h * 256 + part * 64 + 64)
                logits = sbuf[n, rows, :] + bias[h, part * 64 : part * 64 + 64, :]
                powers = jnp.exp2(logits - jnp.max(logits, axis=-1, keepdims=True))
                weights.append(powers.astype(BF16))
        mixed = dot(jnp.concatenate(weights, axis=0), vs[n])
        total = mixed[0:256]
        for h in range(1, HEADS):
            mask = jnp.concatenate([head_of, head_of], axis=1) == h
            total = jnp.where(mask, mixed[h * 256 : h * 256 + 256], total)
        attended = total[:, 0:CH] / total[:, CH : 2 * CH]
        gated = (attended * gs[n]).astype(BF16)
        before = upd[owner * OWN + n % OWN, :, core].reshape(256, CH).astype(F32)
        result = before + dot(gated, ao[...])
        osend[n] = result.astype(BF16).reshape(LINE, 4, 16, CH)
        target = out.at[q * OWN + n % OWN, :, core]
        for d in (2, 1, 3):
            remote(osend.at[n, xs[d]], target, o_send, o_recv, place(z, y, owner), xs[d]).start()

    @pl.loop(OWN, 2 * OWN)
    def _(n):
        attend(n, 1 - core)

    target = out.at[pl.ds(q * OWN, OWN), :, core]
    remote(osend.at[OWN : 2 * OWN, q], target, o_send, o_recv, twin, q).start()

    @pl.loop(0, OWN)
    def _(n):
        attend(n, core)

    pltpu.make_async_copy(osend.at[0:OWN, q], target, o_recv).start()

    settle(out, o_recv)
    settle(osend.at[0:7], o_send)

    @pl.when(core == 0)
    def _():
        settle(esend.at[0:3], e_send.at[0])
        settle(esend.at[0, 0 : 31 * 32], e_send.at[0])
        settle(tsend.at[0, 0 : 63 * 16], t_send.at[0])
        settle(tsend.at[1], t_send.at[1])

    @pl.when(core == 1)
    def _():
        settle(tsend.at[0], e_send.at[2])
        settle(tsend.at[0, 0 : 63 * 16], e_send.at[2])
        settle(tsend.at[0], t_send.at[0])
        settle(tsend.at[1, 0 : 63 * 16], t_send.at[1])

    swap.wait_send()
    for n, (ref, _, _, _) in enumerate(parts):
        settle(ref.at[0, 0:15], p_send.at[n])
        settle(ref.at[0:3], l_send.at[n])


def local(pair_act, valid_count, edge_proj, edge_gate, tri_gate, tri_out, attn_proj, bias_proj, attn_out):
    hbm = pl.BlockSpec(memory_space=pltpu.HBM)
    dma = pltpu.SemaphoreType.DMA
    return pl.pallas_call(
        kernel,
        out_shape=jax.ShapeDtypeStruct((ROWS, 4, 2, 16, CH), BF16),
        in_specs=[hbm] * 9,
        out_specs=pl.BlockSpec(memory_space=pl.ANY),
        scratch_shapes=[
            pltpu.VMEM((1, 1), jnp.int32),
            pltpu.VMEM((ROWS, COLS, CH), BF16),
            pltpu.VMEM((CH, 2 * CH), BF16),
            pltpu.VMEM((CH, 2 * CH), BF16),
            pltpu.VMEM((CH, CH), BF16),
            pltpu.VMEM((CH, CH), BF16),
            pltpu.VMEM((CH, 4 * CH), BF16),
            pltpu.VMEM((HEADS, CH), BF16),
            pltpu.VMEM((CH, CH), BF16),
            pltpu.VMEM((4, 128, CH), BF16),
            pltpu.VMEM((2048, CH), BF16),
            pltpu.VMEM((32 * 36, COLS), F32),
            pltpu.VMEM((4, 1024, COLS), BF16),
            pltpu.VMEM((LINE, 16, 2, 32, COLS), BF16),
            pltpu.VMEM((2, 1024, 128), F32),
            pltpu.VMEM((2, 1024, 128), BF16),
            pltpu.VMEM((CH, 16, 128), BF16),
            pltpu.VMEM((CH * 20, 128), F32),
            pltpu.VMEM((OWN, TOK, CH), F32),
            pltpu.VMEM((LINE, OWN, COLS, CH), BF16),
            pltpu.VMEM((2 * OWN, 16, 2, 16, CH), BF16),
            pltpu.VMEM((OWN, 16, 2, 16, CH), BF16),
            pltpu.VMEM((2 * OWN, 256, CH), BF16),
            pltpu.VMEM((2 * OWN, TOK, CH), BF16),
            pltpu.VMEM((2 * OWN, TOK, 2 * CH), BF16),
            pltpu.VMEM((2 * OWN, 256, CH), F32),
            pltpu.VMEM((LINE, 16, 32, 128), BF16),
            pltpu.VMEM((LINE, 16, 16, 128), BF16),
            pltpu.VMEM((LINE, 16, 16, 128), BF16),
            pltpu.VMEM((2 * OWN, 1024, TOK), F32),
            pltpu.VMEM((LINE, 1024, 128), F32),
            pltpu.VMEM((HEADS, 256, TOK), F32),
            pltpu.VMEM((2 * OWN, LINE, 4, 16, CH), BF16),
            pltpu.SemaphoreType.REGULAR, dma((9,)), dma((3,)), dma((3,)), dma, dma((3,)), dma((3,)), dma((2,)), dma,
            dma((3,)), dma((12,)), dma((3,)), dma((3,)), dma, dma, dma, dma,
        ],
        compiler_params=pltpu.CompilerParams(
            collective_id=0, has_side_effects=True, vmem_limit_bytes=48 * 1024 * 1024
        ),
        name="triangle",
    )(valid_count.reshape(1, 1), *[pltpu.with_memory_space_constraint(a, pltpu.HBM) for a in (pair_act, edge_proj, edge_gate, tri_gate, tri_out, attn_proj, bias_proj.T, attn_out)]).reshape(ROWS, COLS, CH)


def solution(mesh):
    placed = (P("row", "ch", None), P(), P(), P(), P(), P(), P(), P(), P())
    return jax.shard_map(
        local, mesh=mesh, in_specs=placed, out_specs=P("row", "ch", None), check_vma=False
    )
```

```python
import math

import jax
import jax.numpy as jnp
from jax import lax
from jax.experimental import pallas as pl
from jax.experimental.pallas import tpu as pltpu
from jax.sharding import PartitionSpec as P

MESH = pl.DeviceIdType.MESH
EPS = 1e-05
F32 = jnp.float32
BF16 = jnp.bfloat16
LOG2E = math.log2(math.e)
NT = (((1,), (1,)), ((), ()))
NN = (((1,), (0,)), ((), ()))

LINE = 4
ROWS = 16
COLS = 128
CH = 128
TOK = 512
HEADS = 4
HEAD = 32
OWN = 4
DEVICES = 128


OFFSETS = [
    (dz, dy, dc, dx) for dz in range(LINE) for dy in range(LINE) for dc in range(2) for dx in range(LINE)
][1:]


def hops(offset):
    dz, dy, _, dx = offset
    return sum(min(d, LINE - d) for d in (dz, dy, dx))


FAR_FIRST = sorted(OFFSETS, key=hops, reverse=True)


def dot(a, b, dims=NN):
    return lax.dot_general(a, b, dims, preferred_element_type=F32)


def sigmoid(x):
    return 0.5 * jnp.tanh(0.5 * x) + 0.5


def layer_norm(x):
    centre = x - jnp.mean(x, axis=-1, keepdims=True)
    spread = jnp.mean(centre * centre, axis=-1, keepdims=True)
    return centre * lax.rsqrt(spread + EPS)


def kernel(
    count_in, pa_in, ep_in, eg_in, tg_in, to_in, ap_in, bp_in, ao_in,
    out,
    count, pa, ep, eg, tg, to, ap, bp, ao, wt, nrm, ebuf, esend, lr, tst, tsend, trecv, tn, gbuf, a2, upd, an, qs, ks, vs, gs, ba, bb, bc, sbuf, raw, bias, osend,
    ready, load, pa_send, pa_recv, pa_own, e_send, e_recv, t_send, t_recv,
    p_send, p_recv, l_send, l_recv, u_send, u_recv, o_send, o_recv,
):
    r = lax.axis_index("row")
    q = lax.axis_index("ch")
    me = r * LINE + q
    z = lax.div(r, 8)
    y = lax.rem(lax.div(r, 2), 4)
    core = lax.rem(r, 2)

    def place(zz, yy, cc):
        return zz * 8 + yy * 2 + cc

    zs = [lax.rem(z + d, LINE) for d in range(LINE)]
    ys = [lax.rem(y + d, LINE) for d in range(LINE)]
    xs = [lax.rem(q + d, LINE) for d in range(LINE)]
    cores = [core, 1 - core]

    def peer(offset):
        dz, dy, dc, dx = offset
        return place(zs[dz], ys[dy], cores[dc]), xs[dx]

    def remote(src, dst, send, recv, rr, qq):
        return pltpu.make_async_remote_copy(
            src_ref=src, dst_ref=dst, send_sem=send, recv_sem=recv,
            device_id=(rr, qq), device_id_type=MESH,
        )

    def settle(ref, sem):
        pltpu.make_async_copy(ref, ref, sem).wait()

    barrier = pltpu.get_barrier_semaphore()

    plane = [o for o in OFFSETS if o[2] == 0 and o[3] == 0]
    near = [o for o in OFFSETS if o[0] == 0 and o[1] == 0] + plane
    for offset in near:
        rr, qq = peer(offset)
        pl.semaphore_signal(barrier, inc=1, device_id=(rr, qq), device_id_type=MESH)

    loads = [
        pltpu.make_async_copy(src, dst, load.at[n])
        for n, (src, dst) in enumerate(
            [(count_in, count), (ep_in, ep), (eg_in, eg), (pa_in, pa), (tg_in, tg), (to_in, to), (ap_in, ap), (bp_in, bp), (ao_in, ao)]
        )
    ]
    for copy in loads:
        copy.start()

    for copy in loads:
        copy.wait()

    @pl.loop(0, 4)
    def _(part):
        x = pa[pl.ds(part * 4, 4)].reshape(512, CH).astype(F32)
        nrm[pl.ds(pl.multiple_of(part * 512, 512), 512), :] = layer_norm(x).astype(BF16)

    pl.semaphore_wait(barrier, len(near))
    for offset in plane:
        rr, qq = peer(offset)
        pl.semaphore_signal(ready, inc=1, device_id=(rr, qq), device_id_type=MESH)

    spot = lax.broadcasted_iota(jnp.int32, (CH, CH), 0)
    line = spot % 32
    chosen = line * 4 + (spot // 32 + 8 - line // 8 - (line // 2) % 4) % 4
    order = (chosen == lax.broadcasted_iota(jnp.int32, (CH, CH), 1)).astype(BF16)
    for n, ref in enumerate((ep, ep, eg, eg)):
        side = n % 2
        part = dot(order, ref[:, side * CH : side * CH + CH], NT).astype(BF16)
        for m in range(4):
            wt[m, n * 32 : n * 32 + 32, :] = part[m * 32 : m * 32 + 32]
    lane = lax.broadcasted_iota(jnp.int32, (1, 512), 1)

    def edges_of(k):
        weights = wt[lax.rem(z + y + q + k, 4)]
        for part in range(4):
            both = dot(weights, nrm[part * 512 : part * 512 + 512, :], NT)
            row_token = r * ROWS + part * 4 + lane // 128
            col_token = q * COLS + lane % 128
            valid = jnp.where((row_token < count[...]) & (col_token < count[...]), 1.0, 0.0)
            edges = sigmoid(both[64:128]) * both[0:64] * valid
            for i in range(4):
                for side in range(2):
                    ebuf[pl.ds(side * 16 + part * 4 + i, 32, stride=36), :] = edges[
                        side * 32 : side * 32 + 32, i * 128 : i * 128 + 128
                    ]
        for n in range(32):
            esend[k, n * 32 : n * 32 + 32, :] = ebuf[n * 36 : n * 36 + 32, :].astype(BF16)

    for step, k in enumerate((2, 1, 3, 0)):
        edges_of(k)
        if step == 0:
            pl.semaphore_wait(ready, len(plane))
        targets = [o for o in FAR_FIRST if (o[0] + o[1] + o[3]) % 4 == k]

        @pl.when(core == 0)
        def _():
            for offset in targets:
                rr, qq = peer(offset)
                rows = pl.ds(pl.multiple_of(rr * 32, 32), 32)
                remote(esend.at[k, rows], lr.at[q, z * LINE + y, 0], e_send.at[0], e_recv.at[0], rr, qq).start()

        @pl.when(core == 1)
        def _():
            for offset in targets:
                rr, qq = peer(offset)
                rows = pl.ds(pl.multiple_of(rr * 32 + 16, 16), 16)
                remote(
                    esend.at[k, rows], lr.at[q, z * LINE + y, 1, 16:32], e_send.at[1], e_recv.at[1], rr, qq
                ).start()

    @pl.when(core == 0)
    def _():
        own = pl.ds(pl.multiple_of(r * 32, 32), 32)
        pltpu.make_async_copy(esend.at[0, own], lr.at[q, z * LINE + y, 0], e_recv.at[0]).start()

    @pl.when(core == 1)
    def _():
        own = pl.ds(pl.multiple_of(r * 32 + 16, 16), 16)
        pltpu.make_async_copy(esend.at[0, own], lr.at[q, z * LINE + y, 1, 16:32], e_recv.at[1]).start()
        settle(tsend.at[0], e_send.at[1])
        settle(tsend.at[0, 0 : 63 * 16], e_send.at[1])
        for offset in FAR_FIRST:
            rr, qq = peer(offset)
            rows = pl.ds(pl.multiple_of(rr * 32, 32), 16)
            k = (offset[0] + offset[1] + offset[3]) % 4
            remote(
                esend.at[k, rows], lr.at[q, z * LINE + y, 1, 0:16], e_send.at[2], e_recv.at[2], rr, qq
            ).start()
        own = pl.ds(pl.multiple_of(r * 32, 32), 16)
        pltpu.make_async_copy(esend.at[0, own], lr.at[q, z * LINE + y, 1, 0:16], e_recv.at[2]).start()

    pa_copies = []
    for dq in range(1, LINE):
        qq = lax.rem(q + dq, LINE)
        copy = remote(
            pa.at[pl.ds(qq * OWN, OWN)], a2.at[q], pa_send.at[dq - 1], pa_recv.at[dq - 1], r, qq
        )
        copy.start()
        pa_copies.append(copy)
    pa_local = pltpu.make_async_copy(pa.at[pl.ds(q * OWN, OWN)], a2.at[q], pa_own)
    pa_local.start()

    settle(lr.at[:, :, 0], e_recv.at[0])
    settle(lr.at[:, :, 1, 16:32], e_recv.at[1])
    right = jnp.concatenate([lr[k, :, :, 16:32, :].reshape(TOK, COLS) for k in range(LINE)], axis=1)
    for half in range(2):
        if half == 1:
            settle(lr.at[:, :, 1, 0:16], e_recv.at[2])
        left = jnp.concatenate(
            [lr[k, :, half, 0:16, :].reshape(256, COLS) for k in range(LINE)], axis=1
        )
        tri = dot(left, right, NT)
        for jb in range(LINE):
            tst[half, pl.ds(jb, 256, stride=4), :] = tri[:, jb * 128 : jb * 128 + 128]
        tsend[half] = tst[half].astype(BF16)
        for offset in FAR_FIRST:
            if offset[2] == 0:
                zz, yy, qq = zs[offset[0]], ys[offset[1]], xs[offset[3]]
                rows = pl.ds(pl.multiple_of((zz * 16 + yy * 4 + qq) * 16, 16), 16)
                remote(
                    tsend.at[half, rows], trecv.at[me], t_send.at[half], t_recv, place(zz, yy, half), qq
                ).start()
        own = pl.ds(pl.multiple_of((z * 16 + y * 4 + q) * 16, 16), 16)

        @pl.when(core == half)
        def _():
            pltpu.make_async_copy(tsend.at[half, own], trecv.at[me], t_recv).start()

        @pl.when(core != half)
        def _():
            remote(
                tsend.at[half, own], trecv.at[me], t_send.at[half], t_recv, place(z, y, half), q
            ).start()

    spot = lax.broadcasted_iota(jnp.int32, (16, HEADS), 0) % HEADS
    pick = (spot == lax.broadcasted_iota(jnp.int32, (16, HEADS), 1)).astype(BF16)
    bias_w = dot(pick, bp[...]).astype(BF16)
    bias_row = lax.broadcasted_iota(jnp.int32, (16, 128), 0) // HEADS

    pa_local.wait()
    for copy in pa_copies:
        copy.wait()

    @pl.loop(0, OWN)
    def _(jb):
        x = a2[jb].reshape(TOK, CH).astype(F32)
        gbuf[jb] = sigmoid(dot(layer_norm(x).astype(BF16), tg[...]))

    settle(trecv, t_recv)

    def add(part, total):
        return total + jnp.sum(trecv[pl.ds(part * 32, 32)].astype(F32), axis=0)

    mean = lax.fori_loop(0, 4, add, jnp.zeros((16, 128), F32)) * (1.0 / CH)

    def add_square(part, total):
        centre = trecv[pl.ds(part * 32, 32)].astype(F32) - mean[None]
        return total + jnp.sum(centre * centre, axis=0)

    spread = lax.fori_loop(0, 4, add_square, jnp.zeros((16, 128), F32)) * (1.0 / CH)
    gain = lax.rsqrt(spread + EPS)

    @pl.loop(0, 8)
    def _(part):
        block = (trecv[pl.ds(part * 16, 16)].astype(F32) - mean[None]) * gain[None]
        for n in range(16):
            tn[pl.ds(part * 320 + n * 20, 16), :] = block[n]

    u = z + core * (y - z)
    v = y + core * (z - y)
    us = [lax.rem(u + d, LINE) for d in range(LINE)]
    vvs = [lax.rem(v + d, LINE) for d in range(LINE)]
    step_u = 8 - 6 * core
    step_v = 2 + 6 * core
    parts = [(ba, us, vvs, xs), (bb, vvs, us, xs), (bc, xs, us, vvs)]

    def at(n, line, first, second):
        uu, vv, xx = [
            (us[line], vvs[first], xs[second]),
            (us[first], vvs[line], xs[second]),
            (us[first], vvs[second], xs[line]),
        ][n]
        return uu * step_u + vv * step_v + core, xx

    def over_plane(n):
        ref, lines, firsts, seconds = parts[n]
        slot = ref.at[lines[0], firsts[0] * LINE + seconds[0]]
        pairs = [(f, t) for f in range(LINE) for t in range(LINE)][1:]
        for f, t in sorted(pairs, key=lambda p: -min(p[0], LINE - p[0]) - min(p[1], LINE - p[1])):
            remote(slot, slot, p_send.at[n], p_recv.at[n * LINE + f], *at(n, 0, f, t)).start()

    def along_line(n, f):
        ref, lines, firsts, _ = parts[n]
        settle(ref.at[lines[0], 0 : 3 if f == 0 else 4], p_recv.at[n * LINE + f])
        entries = pl.ds(firsts[(LINE - f) % LINE] * LINE, LINE)
        for d in (2, 1, 3):
            slot = ref.at[lines[0], entries]
            remote(slot, slot, l_send.at[n], l_recv.at[n], *at(n, d, 0, 0)).start()

    mine = pl.ds(core * OWN, OWN)
    for jb in range(LINE):
        blocks = [
            tn[pl.ds(il * LINE + jb, 128, stride=20), :].T.astype(BF16) for il in range(OWN)
        ]
        product = dot(jnp.concatenate(blocks, axis=0), to[...])
        x = a2[jb].reshape(TOK, CH).astype(F32)
        updated = (x + gbuf[jb] * product).astype(BF16)
        upd[mine, jb * 4 : jb * 4 + 4] = updated.reshape(OWN, 4, 2, 16, CH)
        normed = layer_norm(updated.astype(F32)).astype(BF16)
        an[:, jb * 4 : jb * 4 + 4] = normed.reshape(OWN, 4, 2, 16, CH)
        biases = dot(bias_w, normed, NT)
        tile = biases[:, 0:128]
        for il in range(1, OWN):
            tile = jnp.where(bias_row == il, biases[:, il * 128 : il * 128 + 128], tile)
        tile = tile.astype(BF16)
        if jb < 2:
            ba[u, v * LINE + q, jb * 16 : jb * 16 + 16, :] = tile
        elif jb == 2:
            bb[v, u * LINE + q] = tile
        else:
            bc[q, u * LINE + v] = tile
        if jb == 1:
            over_plane(0)
    over_plane(1)
    over_plane(2)

    twin = place(z, y, 1 - core)
    swap = remote(upd.at[mine], upd.at[mine], u_send, u_recv, twin, q)
    swap.start()

    head_of = lax.broadcasted_iota(jnp.int32, (256, CH), 1) // HEAD

    def project(n, il):
        half = an[il, :, core].reshape(256, CH)
        qs[n] = (dot(half, ap[:, 0:CH]) * (HEAD**-0.5 * LOG2E)).astype(BF16)
        gs[n] = sigmoid(dot(half, ap[:, 3 * CH : 4 * CH]))
        mixed = dot(an[il].reshape(TOK, CH), ap[:, CH : 3 * CH])
        ks[n] = mixed[:, 0:CH].astype(BF16)
        vs[n, :, 0:CH] = mixed[:, CH : 2 * CH].astype(BF16)
        vs[n, :, CH : 2 * CH] = jnp.ones((TOK, CH), BF16)

    def score(n):
        query = qs[n]
        for pair in range(2):
            masked = [
                jnp.where(head_of == pair * 2 + h, query, jnp.zeros_like(query)) for h in range(2)
            ]
            sbuf[n, pair * 512 : pair * 512 + 512, :] = dot(jnp.concatenate(masked, axis=0), ks[n], NT)

    @pl.loop(0, OWN)
    def _(il):
        project(il, il)

    for f in (0, 1):
        for n in range(3):
            along_line(n, f)
    score(0)
    for n in range(3):
        along_line(n, 3)
    score(1)
    for n in range(3):
        along_line(n, 2)

    @pl.loop(2, OWN)
    def _(n):
        score(n)

    swap.wait_recv()

    @pl.loop(0, OWN)
    def _(il):
        normed = layer_norm(upd[(1 - core) * OWN + il].reshape(TOK, CH).astype(F32)).astype(BF16)
        an[il] = normed.reshape(16, 2, 16, CH)
        project(OWN + il, il)

    @pl.loop(OWN, 2 * OWN)
    def _(n):
        score(n)

    for n, (ref, _, _, _) in enumerate(parts):
        settle(ref.at[0:3], l_recv.at[n])
    key_lane = lax.broadcasted_iota(jnp.int32, (1, TOK), 1)
    key_term = jnp.where(key_lane < count[...], 0.0, -1e9 * LOG2E)
    rows_u = 256 - 192 * core
    rows_v = 64 + 192 * core

    @pl.loop(0, LINE)
    def _(uu):
        for vv in range(LINE):
            for xx in range(LINE):
                rows = pl.ds(pl.multiple_of(uu * rows_u + vv * rows_v + xx * 16, 16), 16)
                pair = ba[uu, vv * LINE + xx]
                tiles = [pair[0:16], pair[16:32], bb[vv, uu * LINE + xx], bc[xx, uu * LINE + vv]]
                for kb, tile in enumerate(tiles):
                    cols = slice(kb * 128, kb * 128 + 128)
                    raw[kb, rows, :] = tile.astype(F32) * LOG2E + key_term[:, cols]

    for kb in range(LINE):
        for h in range(HEADS):
            bias[h, :, kb * 128 : kb * 128 + 128] = raw[kb, pl.ds(h, 256, stride=4), :]

    def attend(n, owner):
        weights = []
        for h in range(HEADS):
            for part in range(4):
                rows = slice(h * 256 + part * 64, h * 256 + part * 64 + 64)
                logits = sbuf[n, rows, :] + bias[h, part * 64 : part * 64 + 64, :]
                powers = jnp.exp2(logits - jnp.max(logits, axis=-1, keepdims=True))
                weights.append(powers.astype(BF16))
        mixed = dot(jnp.concatenate(weights, axis=0), vs[n])
        total = mixed[0:256]
        for h in range(1, HEADS):
            mask = jnp.concatenate([head_of, head_of], axis=1) == h
            total = jnp.where(mask, mixed[h * 256 : h * 256 + 256], total)
        attended = total[:, 0:CH] / total[:, CH : 2 * CH]
        gated = (attended * gs[n]).astype(BF16)
        before = upd[owner * OWN + n % OWN, :, core].reshape(256, CH).astype(F32)
        result = before + dot(gated, ao[...])
        osend[n] = result.astype(BF16).reshape(LINE, 4, 16, CH)
        target = out.at[q * OWN + n % OWN, :, core]
        for d in (2, 1, 3):
            remote(osend.at[n, xs[d]], target, o_send, o_recv, place(z, y, owner), xs[d]).start()

    @pl.loop(0, OWN)
    def _(n):
        attend(n, core)

    target = out.at[pl.ds(q * OWN, OWN), :, core]
    pltpu.make_async_copy(osend.at[0:OWN, q], target, o_recv).start()

    @pl.loop(OWN, 2 * OWN)
    def _(n):
        attend(n, 1 - core)

    remote(osend.at[OWN : 2 * OWN, q], target, o_send, o_recv, twin, q).start()

    settle(out, o_recv)
    settle(osend.at[0:7], o_send)

    @pl.when(core == 0)
    def _():
        settle(esend.at[0:3], e_send.at[0])
        settle(esend.at[0, 0 : 31 * 32], e_send.at[0])
        settle(tsend.at[0, 0 : 63 * 16], t_send.at[0])
        settle(tsend.at[1], t_send.at[1])

    @pl.when(core == 1)
    def _():
        settle(tsend.at[0], e_send.at[2])
        settle(tsend.at[0, 0 : 63 * 16], e_send.at[2])
        settle(tsend.at[0], t_send.at[0])
        settle(tsend.at[1, 0 : 63 * 16], t_send.at[1])

    swap.wait_send()
    for n, (ref, _, _, _) in enumerate(parts):
        settle(ref.at[0, 0:15], p_send.at[n])
        settle(ref.at[0:3], l_send.at[n])


def local(pair_act, valid_count, edge_proj, edge_gate, tri_gate, tri_out, attn_proj, bias_proj, attn_out):
    hbm = pl.BlockSpec(memory_space=pltpu.HBM)
    dma = pltpu.SemaphoreType.DMA
    return pl.pallas_call(
        kernel,
        out_shape=jax.ShapeDtypeStruct((ROWS, 4, 2, 16, CH), BF16),
        in_specs=[hbm] * 9,
        out_specs=pl.BlockSpec(memory_space=pl.ANY),
        scratch_shapes=[
            pltpu.VMEM((1, 1), jnp.int32),
            pltpu.VMEM((ROWS, COLS, CH), BF16),
            pltpu.VMEM((CH, 2 * CH), BF16),
            pltpu.VMEM((CH, 2 * CH), BF16),
            pltpu.VMEM((CH, CH), BF16),
            pltpu.VMEM((CH, CH), BF16),
            pltpu.VMEM((CH, 4 * CH), BF16),
            pltpu.VMEM((HEADS, CH), BF16),
            pltpu.VMEM((CH, CH), BF16),
            pltpu.VMEM((4, 128, CH), BF16),
            pltpu.VMEM((2048, CH), BF16),
            pltpu.VMEM((32 * 36, COLS), F32),
            pltpu.VMEM((4, 1024, COLS), BF16),
            pltpu.VMEM((LINE, 16, 2, 32, COLS), BF16),
            pltpu.VMEM((2, 1024, 128), F32),
            pltpu.VMEM((2, 1024, 128), BF16),
            pltpu.VMEM((CH, 16, 128), BF16),
            pltpu.VMEM((CH * 20, 128), F32),
            pltpu.VMEM((OWN, TOK, CH), F32),
            pltpu.VMEM((LINE, OWN, COLS, CH), BF16),
            pltpu.VMEM((2 * OWN, 16, 2, 16, CH), BF16),
            pltpu.VMEM((OWN, 16, 2, 16, CH), BF16),
            pltpu.VMEM((2 * OWN, 256, CH), BF16),
            pltpu.VMEM((2 * OWN, TOK, CH), BF16),
            pltpu.VMEM((2 * OWN, TOK, 2 * CH), BF16),
            pltpu.VMEM((2 * OWN, 256, CH), F32),
            pltpu.VMEM((LINE, 16, 32, 128), BF16),
            pltpu.VMEM((LINE, 16, 16, 128), BF16),
            pltpu.VMEM((LINE, 16, 16, 128), BF16),
            pltpu.VMEM((2 * OWN, 1024, TOK), F32),
            pltpu.VMEM((LINE, 1024, 128), F32),
            pltpu.VMEM((HEADS, 256, TOK), F32),
            pltpu.VMEM((2 * OWN, LINE, 4, 16, CH), BF16),
            pltpu.SemaphoreType.REGULAR, dma((9,)), dma((3,)), dma((3,)), dma, dma((3,)), dma((3,)), dma((2,)), dma,
            dma((3,)), dma((12,)), dma((3,)), dma((3,)), dma, dma, dma, dma,
        ],
        compiler_params=pltpu.CompilerParams(
            collective_id=0, has_side_effects=True, vmem_limit_bytes=48 * 1024 * 1024
        ),
        name="triangle",
    )(valid_count.reshape(1, 1), *[pltpu.with_memory_space_constraint(a, pltpu.HBM) for a in (pair_act, edge_proj, edge_gate, tri_gate, tri_out, attn_proj, bias_proj.T, attn_out)]).reshape(ROWS, COLS, CH)


def solution(mesh):
    placed = (P("row", "ch", None), P(), P(), P(), P(), P(), P(), P(), P())
    return jax.shard_map(
        local, mesh=mesh, in_specs=placed, out_specs=P("row", "ch", None), check_vma=False
    )
```
